32 devices in a mesh: chan: 8 (over y, x, core), int: 4 (over z).
Axes of the slice: x: 2, y: 2, z: 4, core: 2. Of those that a mesh axis runs over, the one named last changes fastest.
Arguments:
- t_pp: bfloat16 [32768, 2048], P(('chan', 'int')), may hold values from -6 to 6
- interaction: bfloat16 [4, 2048, 2048], P(None, None, 'int'), may hold values from -0.125 to 0.125
- send_order: int32 [32768], P(('chan', 'int')), may hold values from 0 to 1023, as said below
- recv_order: int32 [32768], P(('chan', 'int')), may hold values from 0 to 1023, as said below
- ph_channel: int32 [32768], P('chan'), may hold values from 0 to 4, as said below
- recouple_weight: float32 [32768], P('chan'), may hold values from -1.5 to 1.5
Outputs:
- term_pp: bfloat16 [32768, 2048], P(('chan', 'int'))
The draws below stay inside these ranges and needn't reach their ends.
Inputs may be any that keep to these rules, and one draw needn't show every extreme that they name: `send_order`: within each device's 1024 slots a permutation of its local rows. `recv_order`: within each device's 1024 slots a permutation of its received rows. `ph_channel`: non-decreasing within each device's 1024 slots; the value 4 marks empty slots, which come last; some device has no empty slot.
All inputs are finite; a program needn't handle non-finite values.
Results may differ from the reference program's by a relative error of at most 0.001.
Values may be sent and summed in bfloat16 or wider, within the bound.
No kernel may reach another device: no remote copies, remote signals or barrier semaphores. Data moves between devices by JAX's collectives and lax.ppermute only.
A program may use at most 128 MiB of HBM per device.

```python
import jax
import jax.numpy as jnp
from jax import lax

W = 2048
NCH = 4
R_DEV = 1024
ROWS = 32768
N_CHAN = 8
N_INT = 4


def draw_send_order(key, part):
    block_count = ROWS // R_DEV
    keys = jax.random.split(jax.random.fold_in(key, 3), block_count)
    perms = jax.vmap(lambda one_key: jax.random.permutation(one_key, R_DEV))(keys)
    return perms.reshape(ROWS).astype(jnp.int32)


def draw_recv_order(key, part):
    block_count = ROWS // R_DEV
    keys = jax.random.split(jax.random.fold_in(key, 7), block_count)
    perms = jax.vmap(lambda one_key: jax.random.permutation(one_key, R_DEV))(keys)
    return perms.reshape(ROWS).astype(jnp.int32)


def draw_ph_channel(key, part):
    block_count = ROWS // R_DEV
    first_key, second_key, third_key = jax.random.split(jax.random.fold_in(key, 11), 3)
    live = jax.random.randint(first_key, (block_count,), R_DEV // 4, R_DEV + 1)
    full_block = jax.random.randint(second_key, (), 0, block_count)
    live = jnp.where(jnp.arange(block_count) == full_block, R_DEV, live)
    cuts = jax.random.randint(third_key, (block_count, NCH - 1), 0, R_DEV + 1)
    cuts = jnp.minimum(cuts, live[:, None])
    slots = jnp.arange(R_DEV)
    channel_ids = jnp.sum((cuts[:, None, :] <= slots[None, :, None]).astype(jnp.int32), axis=2)
    channel_ids = jnp.where(slots[None, :] < live[:, None], channel_ids, NCH)
    return channel_ids.reshape(ROWS).astype(jnp.int32)


def level_of(rng, shape, cuts, least, top_value):
    def one(dim, blocks):
        draws = jax.random.uniform(jax.random.fold_in(jax.random.fold_in(rng, 6), dim), (blocks,), jnp.float32, least / len(cuts), top_value / len(cuts))
        return jnp.repeat(jnp.exp(draws), shape[dim] // blocks).reshape((-1,) + (1,) * (len(shape) - dim - 1))

    gain = one(*cuts[0])
    for cut in cuts[1:]:
        gain = gain * one(*cut)
    return gain


def normal_values(key, dims, width, reach, cuts=(), held_as=jnp.bfloat16):
    values = jax.random.normal(key, dims, jnp.float32) * width
    if len(cuts) > 0:
        values = level_of(key, dims, cuts, -0.22, 0.18) * values
    return jnp.clip(values, min=-reach, max=reach).astype(held_as)


def setup_inputs(seed: int = 0) -> dict:
    arg_keys = jax.random.split(jax.random.key(seed), 7)
    return {
        "t_pp": normal_values(arg_keys[0], (ROWS, W), 1.0, 6.0, ((0, 32),)),
        "interaction": normal_values(arg_keys[1], (NCH, W, W), W ** -0.5, 0.125, ((2, 4),)),
        "send_order": draw_send_order(jax.random.fold_in(arg_keys[6], 71), 0),
        "recv_order": draw_recv_order(jax.random.fold_in(arg_keys[6], 71), 0),
        "ph_channel": draw_ph_channel(jax.random.fold_in(arg_keys[6], 71), 0),
        "recouple_weight": jnp.clip(jax.random.uniform(arg_keys[5], (ROWS,), jnp.float32, -1.5, 1.5) * level_of(arg_keys[5], (ROWS,), ((0, 8),), -0.4, 0.0), -1.5, 1.5),
    }


def reference(t_pp, interaction, send_order, recv_order, ph_channel, recouple_weight):
    quota = R_DEV // N_CHAN
    block_count = N_CHAN * N_INT
    position = jnp.arange(ROWS, dtype=jnp.int32)
    block_index = position // R_DEV
    arrived = recv_order.astype(jnp.int32)
    target_chan = block_index // N_INT
    int_index = block_index % N_INT
    source_block = (arrived // quota) * N_INT + int_index
    source_slot = target_chan * quota + arrived % quota
    source = (source_block * R_DEV + send_order[source_block * R_DEV + source_slot]).astype(jnp.int32)
    t_ph = t_pp[source].reshape(block_count, R_DEV, W)
    channel_ids = ph_channel.reshape(block_count, R_DEV)
    weights = recouple_weight.reshape(block_count, R_DEV)

    def one_block(packed):
        amps, ids, scale = packed
        total = jnp.zeros((R_DEV, W), jnp.float32)
        for channel in range(NCH):
            product = jnp.dot(amps, interaction[channel], preferred_element_type=jnp.float32)
            total = total + jnp.where((ids == channel)[:, None], product, jnp.float32(0.0))
        result = jnp.where((ids < NCH)[:, None], scale[:, None] * total, jnp.float32(0.0))
        return result.astype(jnp.bfloat16)

    z_ph = lax.map(one_block, (t_ph, channel_ids, weights)).reshape(ROWS, W)
    return jnp.zeros((ROWS, W), jnp.bfloat16).at[source].set(z_ph)
```

```python
import functools

import jax
import jax.numpy as jnp
from jax import lax
from jax.experimental import pallas as pl
from jax.experimental.pallas import tpu as pltpu
from jax.sharding import PartitionSpec as P

VMEM_BYTES = 48 * 1024 * 1024


def multiply_body(layout, scalars, t_ref, meta_ref, *refs):
    out_ref = refs[-1]
    result = refs[-2][...]
    channel_ids = meta_ref[:, 0:1]
    scale = meta_ref[:, 1:2]
    place, used = 1, 0
    for row_counts in layout:
        channel = scalars[place].astype(jnp.float32)
        place += 1
        product = None
        for count in row_counts:
            first = pl.multiple_of(scalars[place], 256)
            part = jnp.dot(
                t_ref[:, pl.ds(first, count)], refs[used][...], preferred_element_type=jnp.float32
            )
            product = part if product is None else product + part
            place += 1
            used += 1
        result = jnp.where(channel_ids == channel, (scale * product).astype(result.dtype), result)
    out_ref[...] = result


def multiply(out, t_pp, meta, column_block, blocks):
    slots, depth = t_pp.shape
    tile = min(256, slots)
    arrays = [rows for _, parts in blocks for _, rows in parts]
    width = arrays[0].shape[1]
    layout = tuple(tuple(rows.shape[0] for _, rows in parts) for _, parts in blocks)
    scalars = [column_block]
    for channel, parts in blocks:
        scalars.append(channel)
        scalars.extend(first for first, _ in parts)
    scalars = jnp.stack([jnp.asarray(value, jnp.int32) for value in scalars])
    row_total = sum(rows.shape[0] for rows in arrays)
    grid_spec = pltpu.PrefetchScalarGridSpec(
        num_scalar_prefetch=1,
        grid=(slots // tile,),
        in_specs=[
            pl.BlockSpec((tile, depth), lambda i, s: (i, 0)),
            pl.BlockSpec((tile, meta.shape[1]), lambda i, s: (i, 0)),
            *[pl.BlockSpec(rows.shape, lambda i, s: (0, 0)) for rows in arrays],
            pl.BlockSpec((tile, width), lambda i, s: (i, s[0])),
        ],
        out_specs=pl.BlockSpec((tile, width), lambda i, s: (i, s[0])),
    )
    return pl.pallas_call(
        functools.partial(multiply_body, layout),
        grid_spec=grid_spec,
        out_shape=jax.ShapeDtypeStruct(out.shape, out.dtype),
        input_output_aliases={3 + len(arrays): 0},
        cost_estimate=pl.CostEstimate(
            flops=2 * slots * row_total * width,
            bytes_accessed=2 * (slots * depth + row_total * width + 2 * slots * width),
            transcendentals=0,
        ),
        compiler_params=pltpu.CompilerParams(vmem_limit_bytes=VMEM_BYTES),
    )(scalars, t_pp, meta, *arrays, out)


def inverse_take(order, values):
    hit = order[None, :] == jnp.arange(order.shape[0], dtype=order.dtype)[:, None]
    return [jnp.sum(jnp.where(hit, value[None, :], 0.0), axis=1) for value in values]


def row_meta(send_order, recv_order, ph_channel, recouple_weight):
    slots = send_order.shape[0]
    group = lax.axis_size("chan")
    member = lax.axis_index("int") * slots
    ids = lax.dynamic_slice(ph_channel, (member,), (slots,)).astype(jnp.float32)
    scale = lax.dynamic_slice(recouple_weight, (member,), (slots,))
    back = jnp.stack(inverse_take(recv_order, [ids, scale]), axis=0)
    back = back.reshape(2, group, slots // group).transpose(1, 0, 2)
    back = lax.all_to_all(back, "chan", split_axis=0, concat_axis=0, tiled=True)
    back = back.transpose(1, 0, 2).reshape(2, slots)
    ids, scale = inverse_take(send_order, [back[0], back[1]])
    lane = jnp.arange(128)[None, :]
    return jnp.where(lane == 0, ids[:, None], jnp.where(lane == 1, scale[:, None], 0.0))


def general_plan(t_pp, interaction, meta):
    slots, depth = t_pp.shape
    channels, _, width = interaction.shape
    group, members = lax.axis_size("chan"), lax.axis_size("int")
    flat = interaction.reshape(channels * depth, width)
    share = flat.shape[0] // group
    mine = lax.dynamic_slice(flat, (lax.axis_index("chan") * share, 0), (share, width))
    everyone = lax.all_gather(mine, ("chan", "int"), axis=0, tiled=False)
    everyone = everyone.reshape(group, members, share, width)
    out = jnp.zeros((slots, members * width), t_pp.dtype)
    for member in range(members):
        whole = everyone[:, member].reshape(channels, depth, width)
        for channel in range(channels):
            out = multiply(out, t_pp, meta, member, [(channel, [(0, whole[channel])])])
    return out


def grid_plan(t_pp, interaction, meta_of):
    slots, depth = t_pp.shape
    channels, _, width = interaction.shape
    group, members = lax.axis_size("chan"), lax.axis_size("int")
    axes = ("chan", "int")
    c, z = lax.axis_index("chan"), lax.axis_index("int")
    core, chip = c % 2, c // 2
    half = depth // 2

    def at(chan, member):
        return chan * members + member

    along = []
    for chan in range(group):
        for member in range(members):
            target = member - 1 if chan % 2 == 0 else member + 1
            if 0 <= target < members:
                along.append((at(chan, member), at(chan, target)))
    pair = [(at(a, m), at(a, m ^ 1)) for a in range(group) for m in range(members)]
    plane = [
        (at(a, m), at(a ^ (2 if a % 2 == 0 else 4), m)) for a in range(group) for m in range(members)
    ]
    other = [(a, a ^ 1) for a in range(group)]

    def sib(x):
        return lax.ppermute(x, "chan", other)

    flat = interaction.reshape(channels * depth, width)

    def own_rows(channel, first, count):
        return lax.dynamic_slice(flat, (channel * depth + first, 0), (count, width))

    sent = [own_rows(chip, 0, half), own_rows(chip, half, half)]
    steps = []
    for step in range(members - 1):
        sent = [lax.ppermute(x, axes, along) for x in sent]
        steps.append(sent)
    extra = lax.ppermute(own_rows(chip ^ 3, core * half, half), axes, pair)

    met = [[sib(x) for x in got] for got in steps]

    end = (z == 0) | (z == members - 1)
    low = z < members // 2
    down = core == 0

    def pick(wanted_down, a, b):
        return jnp.where(wanted_down == down, a, b)

    slot_rows = [[pick(z % 2 == 0, steps[0][h], met[0][h]) for h in range(2)]]
    for step in (0, 1):
        slot_rows.append(
            [
                pick(
                    low,
                    jnp.where(end, steps[step + 1][h], steps[step][h]),
                    jnp.where(end, met[step + 1][h], met[step][h]),
                )
                for h in range(2)
            ]
        )
    block_of = [z ^ 1, jnp.where(low, 2, 1), jnp.where(low, 3, 0)]

    meta = meta_of()
    out = jnp.zeros((slots, members * width), t_pp.dtype)
    for channel in range(channels):
        out = multiply(out, t_pp, meta, z, [(channel, [(0, interaction[channel])])])

    near = chip ^ (1 + core)
    far = chip ^ (2 - core)
    mine, theirs = core * half, (1 - core) * half
    extra_sib = sib(extra)
    for slot in range(3):
        column = block_of[slot]
        a, b = slot_rows[slot]
        got = [lax.ppermute(x, axes, plane) for x in (a, b)]
        got_sib = [sib(x) for x in got]
        out = multiply(out, t_pp, meta, column, [(chip, [(0, a), (half, b)])])
        out = multiply(out, t_pp, meta, column, [(near, [(0, got[0]), (half, got[1])])])
        out = multiply(out, t_pp, meta, column, [(far, [(0, got_sib[0]), (half, got_sib[1])])])
        if slot == 0:
            across, across_sib = extra, extra_sib
        else:
            across = lax.ppermute(jnp.where(core == 0, got_sib[0], got_sib[1]), axes, plane)
            across_sib = sib(across)
        out = multiply(out, t_pp, meta, column, [(chip ^ 3, [(mine, across), (theirs, across_sib)])])
    return out


def on_device(t_pp, interaction, send_order, recv_order, ph_channel, recouple_weight):
    meta_of = functools.partial(row_meta, send_order, recv_order, ph_channel, recouple_weight)
    planes = lax.axis_size("chan") // 2
    if planes == 4 and lax.axis_size("int") == 4 and interaction.shape[0] == planes:
        return grid_plan(t_pp, interaction, meta_of)
    return general_plan(t_pp, interaction, meta_of())


def solution(mesh):
    in_specs = (
        P(("chan", "int"), None),
        P(None, None, "int"),
        P(("chan", "int")),
        P(("chan", "int")),
        P("chan"),
        P("chan"),
    )
    out_specs = P(("chan", "int"), None)
    return jax.shard_map(
        on_device, mesh=mesh, in_specs=in_specs, out_specs=out_specs, check_vma=False
    )
```

```python
import functools

import jax
import jax.numpy as jnp
from jax import lax
from jax.experimental import pallas as pl
from jax.experimental.pallas import tpu as pltpu
from jax.sharding import PartitionSpec as P

VMEM_BYTES = 64 * 1024 * 1024 - 256 * 1024
IN_SMEM = pl.BlockSpec(memory_space=pltpu.SMEM)
IN_HBM = pl.BlockSpec(memory_space=pl.ANY)
PARAMS = pltpu.CompilerParams(vmem_limit_bytes=VMEM_BYTES)
NO_COST = pl.CostEstimate(flops=1, bytes_accessed=1, transcendentals=0)


def after(arrays, earlier):
    count = len(arrays)

    def body(*refs):
        del refs

    return pl.pallas_call(
        body,
        in_specs=[IN_HBM] * (count + len(earlier)),
        out_specs=[IN_HBM] * count,
        out_shape=[jax.ShapeDtypeStruct(x.shape, x.dtype) for x in arrays],
        input_output_aliases={n: n for n in range(count)},
        cost_estimate=NO_COST,
        compiler_params=PARAMS,
    )(*arrays, *earlier)


def choose(index, choices, earlier, pieces=2):
    count = len(choices)
    height, width = choices[0].shape
    part = height // pieces

    def body(index_ref, *refs):
        out_ref, staged, got, put = refs[-4:]

        def fetch(n, p):
            rows = pl.ds(p * part, part)
            return pltpu.make_async_copy(refs[n].at[rows, :], staged.at[rows, :], got.at[p])

        def store(p):
            rows = pl.ds(p * part, part)
            return pltpu.make_async_copy(staged.at[rows, :], out_ref.at[rows, :], put.at[p])

        for n in range(count):

            @pl.when(index_ref[0] == n)
            def _():
                for p in range(pieces):
                    fetch(n, p).start()

        for p in range(pieces):
            fetch(0, p).wait()
            store(p).start()
        for p in range(pieces):
            store(p).wait()

    return pl.pallas_call(
        body,
        in_specs=[IN_SMEM] + [IN_HBM] * (count + len(earlier)),
        out_specs=IN_HBM,
        out_shape=jax.ShapeDtypeStruct((height, width), choices[0].dtype),
        scratch_shapes=[
            pltpu.VMEM((height, width), choices[0].dtype),
            pltpu.SemaphoreType.DMA((pieces,)),
            pltpu.SemaphoreType.DMA((pieces,)),
        ],
        cost_estimate=NO_COST,
        compiler_params=PARAMS,
    )(index, *choices, *earlier)


def cut(x, index, sizes, earlier):
    def body(index_ref, x_ref, *refs):
        out_ref, staged, sem = refs[-3:]
        rows = pl.ds(pl.multiple_of(index_ref[1], 16), sizes[0])
        columns = pl.ds(pl.multiple_of(index_ref[2], 128), sizes[1])
        fetch = pltpu.make_async_copy(x_ref.at[index_ref[0], rows, columns], staged, sem)
        fetch.start()
        fetch.wait()
        store = pltpu.make_async_copy(staged, out_ref, sem)
        store.start()
        store.wait()

    return pl.pallas_call(
        body,
        in_specs=[IN_SMEM] + [IN_HBM] * (1 + len(earlier)),
        out_specs=IN_HBM,
        out_shape=jax.ShapeDtypeStruct(sizes, x.dtype),
        scratch_shapes=[pltpu.VMEM(sizes, x.dtype), pltpu.SemaphoreType.DMA],
        cost_estimate=NO_COST,
        compiler_params=PARAMS,
    )(jnp.stack([jnp.asarray(n, jnp.int32) for n in index]), x, *earlier)


class Group:
    def __init__(self, blocks, before=None, column=None):
        self.blocks, self.before, self.column = blocks, before, column


def products_body(plan, scalars, *refs):
    layouts, finals, befores, sides, tile, stacked, in_count = plan
    hbm_rows = refs[: 2 * sides]
    place = 2 * sides
    array_count = sum(len(counts) for layout in layouts for counts in layout)
    if stacked:
        arrays = [refs[place].at[n] for n in range(array_count)]
        place += 1
    else:
        arrays = refs[place : place + array_count]
        place += array_count
    before_hbm = []
    for before in befores:
        before_hbm.append(refs[place : place + sides] if before else None)
        place += sides if before else 0
    outs = refs[in_count : in_count + sides * len(layouts)]
    scratch = refs[in_count + sides * len(layouts) :]
    t_refs, meta_refs = scratch[:sides], scratch[sides : 2 * sides]
    held = scratch[2 * sides : 2 * sides + array_count]
    staged, before_ref, t_sems, meta_sems, v_sems, before_sems, out_sems = scratch[2 * sides + array_count :]
    slots = t_refs[0].shape[0]
    width = staged.shape[2]
    tiles = slots // tile
    steps = [(side, i) for side in range(sides) for i in range(tiles)]

    def t_copy(step):
        side, i = steps[step]
        rows = pl.ds(i * tile, tile)
        return pltpu.make_async_copy(hbm_rows[side].at[rows, :], t_refs[side].at[rows, :], t_sems.at[step])

    def meta_copy(side):
        return pltpu.make_async_copy(hbm_rows[sides + side], meta_refs[side], meta_sems.at[side])

    def v_copy(n):
        return pltpu.make_async_copy(arrays[n], held[n], v_sems.at[n])

    def before_copy(g, side):
        rows = pl.ds(side * slots, slots)
        return pltpu.make_async_copy(before_hbm[g][side], before_ref.at[g, rows, :], before_sems.at[g * sides + side])

    def out_copy(g, step):
        side, i = steps[step]
        rows = pl.ds(i * tile, tile)
        target = outs[g * sides + side].at[rows, :]
        if side == 0 and finals[g]:
            columns = pl.ds(pl.multiple_of(scalars[g], 128), width)
            target = outs[g * sides].at[rows, columns]
        return pltpu.make_async_copy(
            staged.at[g, pl.ds(step * tile, tile), :], target, out_sems.at[g * len(steps) + step]
        )

    v_copy(0).start()
    meta_copy(0).start()
    for step in range(tiles):
        t_copy(step).start()
    for n in range(1, array_count):
        v_copy(n).start()
    for step in range(tiles, len(steps)):
        t_copy(step).start()
    if sides == 2:
        meta_copy(1).start()
    for g in range(len(layouts)):
        for side in range(sides if befores[g] else 0):
            before_copy(g, side).start()
    for step, (side, i) in enumerate(steps):
        if i == 0:
            meta_copy(side).wait()
            for later in range(tiles):
                t_copy(step + later).wait()
            if step == 0:
                for n in range(array_count):
                    v_copy(n).wait()
            for g in range(len(layouts)):
                if befores[g]:
                    before_copy(g, side).wait()
        rows = pl.ds(i * tile, tile)
        here = pl.ds(step * tile, tile)
        at, used = len(layouts), 0
        for g, layout in enumerate(layouts):
            total = None
            for counts in layout:
                channel = scalars[at].astype(jnp.float32)
                at += 1
                scale = jnp.where(meta_refs[side][rows, 0:1] == channel, meta_refs[side][rows, 1:2], 0.0)
                product = None
                for count in counts:
                    part = jnp.dot(
                        t_refs[side][rows, pl.ds(pl.multiple_of(scalars[at], 256), count)],
                        held[used][...],
                        preferred_element_type=jnp.float32,
                    )
                    product = part if product is None else product + part
                    at += 1
                    used += 1
                total = scale * product if total is None else total + scale * product
            if befores[g]:
                total = total + before_ref[g, here, :].astype(jnp.float32)
            staged[g, here, :] = total.astype(staged.dtype)
        if i == tiles - 1:
            for g in range(len(layouts)):
                for done in range(step - tiles + 1, step + 1):
                    out_copy(g, done).start()
    for g in range(len(layouts)):
        for step in range(len(steps)):
            out_copy(g, step).wait()


def products(t_rows, metas, groups, earlier, out=None, result=None):
    sides = len(t_rows)
    slots, depth = t_rows[0].shape
    dtype = t_rows[0].dtype
    tile = min(512, slots)
    stacked = not isinstance(groups[0].blocks[0][1], list)
    if stacked:
        arrays = [groups[0].blocks[0][1]]
        width = arrays[0].shape[2]
        held = [pltpu.VMEM(arrays[0].shape[1:], dtype)] * len(groups[0].blocks)
        layouts = (((depth,),) * len(groups[0].blocks),)
        firsts = [[(channel, [0]) for channel, _ in groups[0].blocks]]
    else:
        arrays = [x for group in groups for _, parts in group.blocks for _, x in parts]
        width = arrays[0].shape[1]
        held = [pltpu.VMEM(x.shape, dtype) for x in arrays]
        layouts = tuple(
            tuple(tuple(x.shape[0] for _, x in parts) for _, parts in group.blocks) for group in groups
        )
        firsts = [[(channel, [n for n, _ in parts]) for channel, parts in group.blocks] for group in groups]
    scalars = [0 if group.column is None else group.column for group in groups]
    for group in firsts:
        for channel, starts in group:
            scalars.extend([channel, *starts])
    scalars = jnp.stack([jnp.asarray(value, jnp.int32) for value in scalars])
    operands = [*t_rows, *metas, *arrays]
    for group in groups:
        operands.extend(group.before or ())
    aliases, totals = {}, []
    for n, group in enumerate(groups):
        totals.extend([jax.ShapeDtypeStruct((slots, width), dtype)] * sides)
        if group.column is not None:
            totals[n * sides] = jax.ShapeDtypeStruct(result, dtype)
            if out is not None:
                aliases[1 + len(operands)] = n * sides
                operands.append(out)
    operands.extend(earlier)
    steps = sides * (slots // tile)
    finals = tuple(group.column is not None for group in groups)
    befores = tuple(group.before is not None for group in groups)
    plan = (layouts, finals, befores, sides, tile, stacked, len(operands))
    height = sides * slots
    sums = pl.pallas_call(
        functools.partial(products_body, plan),
        in_specs=[IN_SMEM] + [IN_HBM] * len(operands),
        out_specs=[IN_HBM] * len(totals),
        out_shape=totals,
        input_output_aliases=aliases,
        scratch_shapes=[
            *[pltpu.VMEM((slots, depth), dtype)] * sides,
            *[pltpu.VMEM(metas[0].shape, metas[0].dtype)] * sides,
            *held,
            pltpu.VMEM((len(groups), height, width), dtype),
            pltpu.VMEM((len(groups), height if any(befores) else 16, width), dtype),
            pltpu.SemaphoreType.DMA((steps,)),
            pltpu.SemaphoreType.DMA((sides,)),
            pltpu.SemaphoreType.DMA((len(held),)),
            pltpu.SemaphoreType.DMA((sides * len(groups),)),
            pltpu.SemaphoreType.DMA((steps * len(groups),)),
        ],
        cost_estimate=NO_COST,
        compiler_params=PARAMS,
    )(scalars, *operands)
    return [sums[n * sides : (n + 1) * sides] for n in range(len(groups))]


def place(out, columns, arrays, earlier):
    count, pieces = len(arrays), 2
    slots, width = arrays[0].shape
    part = slots // pieces

    def body(columns_ref, *refs):
        out_ref, staged, got, put = refs[-4:]

        def fetch(n, p):
            rows = pl.ds(p * part, part)
            return pltpu.make_async_copy(refs[n].at[rows, :], staged.at[n, rows, :], got.at[n * pieces + p])

        def store(n, p):
            rows = pl.ds(p * part, part)
            columns = pl.ds(pl.multiple_of(columns_ref[n], 128), width)
            return pltpu.make_async_copy(staged.at[n, rows, :], out_ref.at[rows, columns], put.at[n * pieces + p])

        every = [(n, p) for n in range(count) for p in range(pieces)]
        for n, p in every:
            fetch(n, p).start()
        for n, p in every:
            fetch(n, p).wait()
            store(n, p).start()
        for n, p in every:
            store(n, p).wait()

    return pl.pallas_call(
        body,
        in_specs=[IN_SMEM] + [IN_HBM] * (count + 1 + len(earlier)),
        out_specs=IN_HBM,
        out_shape=jax.ShapeDtypeStruct(out.shape, out.dtype),
        input_output_aliases={1 + count: 0},
        scratch_shapes=[
            pltpu.VMEM((count, slots, width), out.dtype),
            pltpu.SemaphoreType.DMA((count * pieces,)),
            pltpu.SemaphoreType.DMA((count * pieces,)),
        ],
        cost_estimate=NO_COST,
        compiler_params=PARAMS,
    )(jnp.stack(columns).astype(jnp.int32), *arrays, out, *earlier)


def inverse_take(order, values):
    hit = order[None, :] == jnp.arange(order.shape[0], dtype=order.dtype)[:, None]
    return [jnp.sum(jnp.where(hit, value[None, :], 0.0), axis=1) for value in values]


def meta_to_owners(recv_order, ph_channel, recouple_weight, earlier=None):
    slots = recv_order.shape[0]
    group = lax.axis_size("chan")
    member = lax.axis_index("int") * slots
    ids = lax.dynamic_slice(ph_channel, (member,), (slots,)).astype(jnp.float32)
    scale = lax.dynamic_slice(recouple_weight, (member,), (slots,))
    back = jnp.stack(inverse_take(recv_order, [ids, scale]), axis=0)
    back = back.reshape(2, group, slots // group).transpose(1, 0, 2)
    if earlier is not None:
        (back,) = after([back], [earlier])
    return lax.all_to_all(back, "chan", split_axis=0, concat_axis=0, tiled=True)


def meta_of_rows(send_order, returned):
    back = returned.transpose(1, 0, 2).reshape(2, -1)
    ids, scale = inverse_take(send_order, [back[0], back[1]])
    lane = jnp.arange(128)[None, :]
    return jnp.where(lane == 0, ids[:, None], jnp.where(lane == 1, scale[:, None], 0.0))


def general_plan(t_pp, interaction, meta):
    slots, depth = t_pp.shape
    channels, _, width = interaction.shape
    group, members = lax.axis_size("chan"), lax.axis_size("int")
    flat = interaction.reshape(channels * depth, width)
    share = flat.shape[0] // group
    mine = lax.dynamic_slice(flat, (lax.axis_index("chan") * share, 0), (share, width))
    everyone = lax.all_gather(mine, ("chan", "int"), axis=0, tiled=False)
    everyone = everyone.reshape(group, members, share, width)
    out = None
    for member in range(members):
        whole = everyone[:, member].reshape(channels, depth, width)
        column, shape = jnp.int32(member * width), (slots, members * width)
        group_of = Group([(channel, whole) for channel in range(channels)], column=column)
        ((out,),) = products([t_pp], [meta], [group_of], [], out=out, result=shape)
    return out


def grid_plan(t_pp, interaction, meta_sent, meta_got):
    slots, depth = t_pp.shape
    channels, _, width = interaction.shape
    group, members = lax.axis_size("chan"), lax.axis_size("int")
    axes = ("chan", "int")
    c, z = lax.axis_index("chan"), lax.axis_index("int")
    core, chip = c % 2, c // 2
    half, part = depth // 2, width // 2
    shape = (slots, members * width)

    def at(chan, member):
        return chan * members + member

    def along(pairs):
        return [(at(a, m), at(a, n)) for a in range(group) for m, n in pairs]

    outer = along([(0, 1), (1, 0), (2, 3), (3, 2)])
    middle = along([(1, 2), (2, 1)])
    outwards = along([(1, 0), (2, 3)])
    sideways = [(a, a ^ 2) for a in range(group)]
    upwards = [(a, a ^ 4) for a in range(group)]
    other = [(a, a ^ 1) for a in range(group)]

    def step(x, pairs):
        return lax.ppermute(x, axes, pairs)

    def by_x(x):
        return lax.ppermute(x, "chan", sideways)

    def by_y(x):
        return lax.ppermute(x, "chan", upwards)

    def sib(x):
        return lax.ppermute(x, "chan", other)

    end = ((z == 0) | (z == members - 1)).astype(jnp.int32).reshape(1)
    low = z < members // 2
    column_of = [(z ^ 1) * width, jnp.where(low, 2, 1) * width, jnp.where(low, 3, 0) * width]
    mine, theirs = core * part, (1 - core) * part

    def quarter(channel, a, b):
        return (channel, [(0, a), (half, b)])

    def own_rows(channel, first, earlier):
        return cut(interaction, (channel, first, core * part), (half, part), earlier)

    own_a = lax.dynamic_slice(interaction, (chip, 0, core * part), (1, half, part)).reshape(half, part)
    p1a, p2a = step(own_a, outer), step(own_a, middle)
    own_b = own_rows(chip, half, [own_a])
    p1b, p2b = step(own_b, outer), step(own_b, middle)
    other_t = sib(t_pp)
    returned = meta_sent(own_b)

    p1a, p2a = after([p1a, p2a], [returned])
    x1a, y1a, p3a, p4a = by_x(p1a), by_y(p1a), step(p2a, outwards), step(p1a, middle)
    (meta,) = after([meta_got(returned)], [p1a])
    other_meta = sib(meta)
    extra_a = own_rows(chip ^ 3, 0, [meta])
    extra_b = own_rows(chip ^ 3, half, [extra_a])

    p1b, p2b = after([p1b, p2b], [extra_b])
    x1b, y1b, p3b, p4b = by_x(p1b), by_y(p1b), step(p2b, outwards), step(p1b, middle)
    own = Group([(channel, interaction) for channel in range(channels)], column=z * width)
    ((out,),) = products([t_pp], [meta], [own], [p1b], result=shape)

    x1a, y1a, p3a, p4a = after([x1a, y1a, p3a, p4a], [out])
    s2a = choose(end, [p2a, p3a], [x1a])
    x2a, y2a, p5a = by_x(s2a), by_y(s2a), step(p4a, outwards)

    x1b, y1b, p3b, p4b = after([x1b, y1b, p3b, p4b], [s2a])
    s2b = choose(end, [p2b, p3b], [x1b])
    x2b, y2b, p5b = by_x(s2b), by_y(s2b), step(p4b, outwards)
    x2a, y2a = after([x2a, y2a], [s2b])
    d2x = by_x(y2a)
    t_rows = [t_pp, other_t]
    metas = [meta, other_meta]
    blocks = [quarter(chip, p1a, p1b), quarter(chip ^ 1, x1a, x1b), quarter(chip ^ 2, y1a, y1b)]
    (sum1,) = products(t_rows, metas, [Group(blocks)], [x2a])

    p5a, x2b, y2b = after([p5a, x2b, y2b], [sum1[0]])
    d2y = by_y(x2b)
    s3a = choose(end, [p4a, p5a], [x2b])
    x3a, y3a = by_x(s3a), by_y(s3a)
    ea = step(extra_a, outer)

    (p5b,) = after([p5b], [s3a])
    s3b = choose(end, [p4b, p5b], [p5b])
    x3b, y3b = by_x(s3b), by_y(s3b)
    eb = step(extra_b, outer)
    d2x, d2y = after([d2x, d2y], [s3b])
    blocks = [
        quarter(chip, s2a, s2b),
        quarter(chip ^ 1, x2a, x2b),
        quarter(chip ^ 2, y2a, y2b),
        quarter(chip ^ 3, d2x, d2y),
    ]
    (out, rest2), sum3 = products(
        t_rows, metas, [Group(blocks, column=column_of[1] + mine), Group([quarter(chip, s3a, s3b)])],
        [d2x], out=out, result=shape,
    )

    x3a, y3a = after([x3a, y3a], [out])
    d3x = by_x(y3a)
    ea, x3b, y3b, eb = after([ea, x3b, y3b, eb], [x3a])
    d3y = by_y(x3b)
    back2 = sib(rest2)
    blocks = [quarter(chip ^ 1, x3a, x3b), quarter(chip ^ 2, y3a, y3b)]
    sum3, (out, rest1) = products(
        t_rows,
        metas,
        [Group(blocks, before=sum3), Group([quarter(chip ^ 3, ea, eb)], before=sum1, column=column_of[0] + mine)],
        [x3b],
        out=out,
        result=shape,
    )
    back1 = sib(rest1)

    d3x, d3y = after([d3x, d3y], [out])
    ((out, rest3),) = products(
        t_rows, metas, [Group([quarter(chip ^ 3, d3x, d3y)], before=sum3, column=column_of[2] + mine)],
        [d3x], out=out, result=shape,
    )
    back3 = sib(rest3)
    columns = [start + theirs for start in column_of]
    return place(out, columns, [back1, back2, back3], [])


def on_device(t_pp, interaction, send_order, recv_order, ph_channel, recouple_weight):
    sent = functools.partial(meta_to_owners, recv_order, ph_channel, recouple_weight)
    got = functools.partial(meta_of_rows, send_order)
    planes = lax.axis_size("chan") // 2
    if planes == 4 and lax.axis_size("int") == 4 and interaction.shape[0] == planes:
        return grid_plan(t_pp, interaction, sent, got)
    return general_plan(t_pp, interaction, got(sent()))


def solution(mesh):
    in_specs = (
        P(("chan", "int"), None),
        P(None, None, "int"),
        P(("chan", "int")),
        P(("chan", "int")),
        P("chan"),
        P("chan"),
    )
    out_specs = P(("chan", "int"), None)
    return jax.shard_map(
        on_device, mesh=mesh, in_specs=in_specs, out_specs=out_specs, check_vma=False
    )
```

```python
import functools

import jax
import jax.numpy as jnp
from jax import lax
from jax.experimental import pallas as pl
from jax.experimental.pallas import tpu as pltpu
from jax.sharding import PartitionSpec as P

VMEM_BYTES = 64 * 1024 * 1024 - 256 * 1024
IN_SMEM = pl.BlockSpec(memory_space=pltpu.SMEM)
IN_HBM = pl.BlockSpec(memory_space=pl.ANY)
PARAMS = pltpu.CompilerParams(vmem_limit_bytes=VMEM_BYTES)
NO_COST = pl.CostEstimate(flops=1, bytes_accessed=1, transcendentals=0)


def after(arrays, earlier):
    count = len(arrays)

    def body(*refs):
        del refs

    return pl.pallas_call(
        body,
        in_specs=[IN_HBM] * (count + len(earlier)),
        out_specs=[IN_HBM] * count,
        out_shape=[jax.ShapeDtypeStruct(x.shape, x.dtype) for x in arrays],
        input_output_aliases={n: n for n in range(count)},
        cost_estimate=NO_COST,
        compiler_params=PARAMS,
    )(*arrays, *earlier)


class Group:
    def __init__(self, blocks, before=None, column=None):
        self.blocks, self.before, self.column = blocks, before, column


def products_body(plan, scalars, *refs):
    layouts, places, finals, befores, sides, tile, stacked, in_count = plan
    hbm_rows = refs[: 2 * sides]
    place = 2 * sides
    array_count = sum(len(counts) for layout in layouts for counts in layout)
    if stacked:
        arrays = [refs[place].at[n] for n in range(array_count)]
        place += 1
    else:
        arrays = refs[place : place + array_count]
        place += array_count
    before_hbm = []
    for before in befores:
        before_hbm.append(refs[place : place + sides] if before else None)
        place += sides if before else 0
    outs = refs[in_count : in_count + sides * len(layouts)]
    scratch = refs[in_count + sides * len(layouts) :]
    t_refs, meta_refs = scratch[:sides], scratch[sides : 2 * sides]
    held = scratch[2 * sides : 2 * sides + array_count]
    staged, before_ref, t_sems, meta_sems, v_sems, before_sems, out_sems = scratch[2 * sides + array_count :]
    slots = t_refs[0].shape[0]
    width = staged.shape[2]
    tiles = slots // tile
    steps = [(side, i) for side in range(sides) for i in range(tiles)]

    def t_copy(step):
        side, i = steps[step]
        rows = pl.ds(i * tile, tile)
        return pltpu.make_async_copy(hbm_rows[side].at[rows, :], t_refs[side].at[rows, :], t_sems.at[step])

    def meta_copy(side):
        return pltpu.make_async_copy(hbm_rows[sides + side], meta_refs[side], meta_sems.at[side])

    def v_copy(n):
        return pltpu.make_async_copy(arrays[n], held[n], v_sems.at[n])

    def before_copy(g, side):
        rows = pl.ds(side * slots, slots)
        return pltpu.make_async_copy(before_hbm[g][side], before_ref.at[g, rows, :], before_sems.at[g * sides + side])

    def out_copy(g, step):
        side, i = steps[step]
        rows = pl.ds(i * tile, tile)
        if side == 0 and finals[g] is not None:
            first = next(n for n in range(len(finals)) if finals[n] is not None)
            columns = pl.ds(pl.multiple_of(scalars[finals[g]], 128), width)
            target = outs[first * sides].at[rows, columns]
        else:
            target = outs[g * sides + side].at[rows, :]
        return pltpu.make_async_copy(
            staged.at[g, pl.ds(step * tile, tile), :], target, out_sems.at[g * len(steps) + step]
        )

    v_copy(0).start()
    meta_copy(0).start()
    for step in range(tiles):
        t_copy(step).start()
    for n in range(1, array_count):
        v_copy(n).start()
    for step in range(tiles, len(steps)):
        t_copy(step).start()
    if sides == 2:
        meta_copy(1).start()
    for g in range(len(layouts)):
        for side in range(sides if befores[g] else 0):
            before_copy(g, side).start()
    for step, (side, i) in enumerate(steps):
        if i == 0:
            meta_copy(side).wait()
            for later in range(tiles):
                t_copy(step + later).wait()
            if step == 0:
                for n in range(array_count):
                    v_copy(n).wait()
            for g in range(len(layouts)):
                if befores[g]:
                    before_copy(g, side).wait()
        rows = pl.ds(i * tile, tile)
        here = pl.ds(step * tile, tile)
        used = 0
        for g, layout in enumerate(layouts):
            total = None
            for counts, (at, starts) in zip(layout, places[g]):
                channel = (jnp.int32(at) if stacked else scalars[at]).astype(jnp.float32)
                scale = jnp.where(meta_refs[side][rows, 0:1] == channel, meta_refs[side][rows, 1:2], 0.0)
                product = None
                for count, first in zip(counts, starts):
                    part = jnp.dot(
                        t_refs[side][rows, first : first + count],
                        held[used][...],
                        preferred_element_type=jnp.float32,
                    )
                    product = part if product is None else product + part
                    used += 1
                total = scale * product if total is None else total + scale * product
            if befores[g]:
                total = total + before_ref[g, here, :].astype(jnp.float32)
            staged[g, here, :] = total.astype(staged.dtype)
        if i == tiles - 1:
            for g in range(len(layouts)):
                for done in range(step - tiles + 1, step + 1):
                    out_copy(g, done).start()
    for g in range(len(layouts)):
        for step in range(len(steps)):
            out_copy(g, step).wait()


def products(table, t_rows, metas, groups, earlier, out=None, result=None):
    sides = len(t_rows)
    slots, depth = t_rows[0].shape
    dtype = t_rows[0].dtype
    tile = min(512, slots)
    stacked = not isinstance(groups[0].blocks[0][1], list)
    if stacked:
        arrays = [groups[0].blocks[0][1]]
        width = arrays[0].shape[2]
        held = [pltpu.VMEM(arrays[0].shape[1:], dtype)] * len(groups[0].blocks)
        layouts = (((depth,),) * len(groups[0].blocks),)
        places = (tuple((channel, (0,)) for channel, _ in groups[0].blocks),)
    else:
        arrays = [x for group in groups for _, parts in group.blocks for _, x in parts]
        width = arrays[0].shape[1]
        held = [pltpu.VMEM(x.shape, dtype) for x in arrays]
        layouts = tuple(
            tuple(tuple(x.shape[0] for _, x in parts) for _, parts in group.blocks) for group in groups
        )
        places = tuple(
            tuple((channel, tuple(n for n, _ in parts)) for channel, parts in group.blocks) for group in groups
        )
    operands = [*t_rows, *metas, *arrays]
    for group in groups:
        operands.extend(group.before or ())
    aliases, totals = {}, []
    for n, group in enumerate(groups):
        totals.extend([jax.ShapeDtypeStruct((slots, width), dtype)] * sides)
        if group.column is not None and result is not None:
            totals[n * sides] = jax.ShapeDtypeStruct(result, dtype)
            result = None
            if out is not None:
                aliases[1 + len(operands)] = n * sides
                operands.append(out)
        elif group.column is not None:
            totals[n * sides] = jax.ShapeDtypeStruct((16, width), dtype)
    operands.extend(earlier)
    steps = sides * (slots // tile)
    finals = tuple(group.column for group in groups)
    befores = tuple(group.before is not None for group in groups)
    plan = (layouts, places, finals, befores, sides, tile, stacked, len(operands))
    height = sides * slots
    sums = pl.pallas_call(
        functools.partial(products_body, plan),
        in_specs=[IN_SMEM] + [IN_HBM] * len(operands),
        out_specs=[IN_HBM] * len(totals),
        out_shape=totals,
        input_output_aliases=aliases,
        scratch_shapes=[
            *[pltpu.VMEM((slots, depth), dtype)] * sides,
            *[pltpu.VMEM(metas[0].shape, metas[0].dtype)] * sides,
            *held,
            pltpu.VMEM((len(groups), height, width), dtype),
            pltpu.VMEM((len(groups), height if any(befores) else 16, width), dtype),
            pltpu.SemaphoreType.DMA((steps,)),
            pltpu.SemaphoreType.DMA((sides,)),
            pltpu.SemaphoreType.DMA((len(held),)),
            pltpu.SemaphoreType.DMA((sides * len(groups),)),
            pltpu.SemaphoreType.DMA((steps * len(groups),)),
        ],
        cost_estimate=NO_COST,
        compiler_params=PARAMS,
    )(table, *operands)
    return [sums[n * sides : (n + 1) * sides] for n in range(len(groups))]


def place(table, out, columns, arrays, earlier):
    count, pieces = len(arrays), 2
    slots, width = arrays[0].shape
    part = slots // pieces

    def body(table_ref, *refs):
        out_ref, staged, got, put = refs[-4:]

        def fetch(n, p):
            rows = pl.ds(p * part, part)
            return pltpu.make_async_copy(refs[n].at[rows, :], staged.at[n, rows, :], got.at[n * pieces + p])

        def store(n, p):
            rows = pl.ds(p * part, part)
            there = pl.ds(pl.multiple_of(table_ref[columns[n]], 128), width)
            return pltpu.make_async_copy(staged.at[n, rows, :], out_ref.at[rows, there], put.at[n * pieces + p])

        every = [(n, p) for n in range(count) for p in range(pieces)]
        for n, p in every:
            fetch(n, p).start()
        for n, p in every:
            fetch(n, p).wait()
            store(n, p).start()
        for n, p in every:
            store(n, p).wait()

    return pl.pallas_call(
        body,
        in_specs=[IN_SMEM] + [IN_HBM] * (count + 1 + len(earlier)),
        out_specs=IN_HBM,
        out_shape=jax.ShapeDtypeStruct(out.shape, out.dtype),
        input_output_aliases={1 + count: 0},
        scratch_shapes=[
            pltpu.VMEM((count, slots, width), out.dtype),
            pltpu.SemaphoreType.DMA((count * pieces,)),
            pltpu.SemaphoreType.DMA((count * pieces,)),
        ],
        cost_estimate=NO_COST,
        compiler_params=PARAMS,
    )(table, *arrays, out, *earlier)


def inverse_take(order, values):
    hit = order[None, :] == jnp.arange(order.shape[0], dtype=order.dtype)[:, None]
    return [jnp.sum(jnp.where(hit, value[None, :], 0.0), axis=1) for value in values]


def meta_to_send(recv_order, ph_channel, recouple_weight, earlier=None):
    slots = recv_order.shape[0]
    group = lax.axis_size("chan")
    member = lax.axis_index("int") * slots
    ids = lax.dynamic_slice(ph_channel, (member,), (slots,)).astype(jnp.float32)
    scale = lax.dynamic_slice(recouple_weight, (member,), (slots,))
    back = jnp.stack(inverse_take(recv_order, [ids, scale]), axis=0)
    back = back.reshape(2, group, slots // group).transpose(1, 0, 2)
    return back if earlier is None else after([back], [earlier])[0]


def meta_over(back):
    return lax.all_to_all(back, "chan", split_axis=0, concat_axis=0, tiled=True)


def meta_of_rows(send_order, returned):
    back = returned.transpose(1, 0, 2).reshape(2, -1)
    ids, scale = inverse_take(send_order, [back[0], back[1]])
    lane = jnp.arange(128)[None, :]
    return jnp.where(lane == 0, ids[:, None], jnp.where(lane == 1, scale[:, None], 0.0))


def general_plan(t_pp, interaction, meta):
    slots, depth = t_pp.shape
    channels, _, width = interaction.shape
    group, members = lax.axis_size("chan"), lax.axis_size("int")
    flat = interaction.reshape(channels * depth, width)
    share = flat.shape[0] // group
    mine = lax.dynamic_slice(flat, (lax.axis_index("chan") * share, 0), (share, width))
    everyone = lax.all_gather(mine, ("chan", "int"), axis=0, tiled=False)
    everyone = everyone.reshape(group, members, share, width)
    out = None
    for member in range(members):
        whole = everyone[:, member].reshape(channels, depth, width)
        group_of = Group([(channel, whole) for channel in range(channels)], column=0)
        table = jnp.full((1,), member * width, jnp.int32)
        ((out,),) = products(table, [t_pp], [meta], [group_of], [], out=out, result=(slots, members * width))
    return out


def grid_plan(t_pp, interaction, meta_sent, meta_over, meta_got):
    slots, depth = t_pp.shape
    channels, _, width = interaction.shape
    group, members = lax.axis_size("chan"), lax.axis_size("int")
    axes = ("chan", "int")
    c, z = lax.axis_index("chan"), lax.axis_index("int")
    core, chip = c % 2, c // 2
    half, part = depth // 2, width // 2
    shape = (slots, members * width)

    def at(chan, member):
        return chan * members + member

    def along(pairs):
        return [(at(a, m), at(a, n)) for a in range(group) for m, n in pairs]

    outer = along([(0, 1), (1, 0), (2, 3), (3, 2)])
    middle = along([(1, 2), (2, 1)])
    outwards = along([(1, 0), (2, 3)])
    near_pairs = [(a, a ^ (4 if a % 2 else 2)) for a in range(group)]
    far_pairs = [(a, a ^ (2 if a % 2 else 4)) for a in range(group)]
    other = [(a, a ^ 1) for a in range(group)]

    def step(x, pairs):
        return lax.ppermute(x, axes, pairs)

    def by_near(x):
        return lax.ppermute(x, "chan", near_pairs)

    def by_far(x):
        return lax.ppermute(x, "chan", far_pairs)

    def sib(x):
        return lax.ppermute(x, "chan", other)

    end = (z == 0) | (z == members - 1)
    low = z < members // 2
    mine, theirs = core * part, (1 - core) * part
    starts = [(z ^ 1) * width, jnp.where(low, 2, 1) * width, jnp.where(low, 3, 0) * width]
    table = [chip, chip ^ (1 + core), chip ^ (2 - core), chip ^ 3] + [z * width] + [n + mine for n in starts] + [n + theirs for n in starts]
    table = jnp.stack(table).astype(jnp.int32)
    own_column, columns, other_columns = 4, (5, 6, 7), (8, 9, 10)

    def quarter(n, x):
        return (n, [(0, x)])

    def own_rows(channel):
        rows = lax.dynamic_slice(interaction, (channel, 0, core * part), (1, depth, part))
        return rows.reshape(depth, part)

    (own,) = after([own_rows(chip)], [])
    p1, p2 = step(own, outer), step(own, middle)
    other_t = sib(t_pp)
    fence = sib(own[:16])
    meta = meta_got(meta_over(meta_sent(fence)))
    (later,) = after([table], [meta])
    extra = own_rows(later[3])
    meta, extra = after([meta, extra], [own])

    p1, p2, other_t = after([p1, p2, other_t], [meta])
    near1, p3, far1, p4 = by_near(p1), step(p2, outwards), by_far(p1), step(p1, middle)
    other_meta = sib(meta)
    local = Group([(channel, interaction) for channel in range(channels)], column=own_column)
    ((out,),) = products(table, [t_pp], [meta], [local], [p1], result=shape)

    near1, far1, p3, other_meta = after([near1, far1, p3, other_meta], [out])
    s2 = jnp.where(end, p3, p2)
    far2, near2 = by_far(s2), by_near(s2)
    (p4,) = after([p4], [s2])
    p5 = step(p4, outwards)
    t_rows = [t_pp, other_t]
    metas = [meta, other_meta]
    (sum1,) = products(table, t_rows, metas, [Group([quarter(0, p1), quarter(1, near1), quarter(2, far1)])], [p4])

    far2, near2, p5 = after([far2, near2, p5], [sum1[0]])
    across2 = by_near(far2)
    s3 = jnp.where(end, p5, p4)
    (extra,) = after([extra], [s3])
    far3, e, near3 = by_far(s3), step(extra, outer), by_near(s3)
    sum2, sum3 = products(
        table, t_rows, metas,
        [Group([quarter(0, s2), quarter(1, near2), quarter(2, far2)]), Group([quarter(0, s3)])],
        [extra],
    )
    across2, e = after([across2, e], [sum2[0]])
    (out, rest1), (_, rest2) = products(
        table, t_rows, metas,
        [
            Group([quarter(3, e)], before=sum1, column=columns[0]),
            Group([quarter(3, across2)], before=sum2, column=columns[1]),
        ],
        [across2], out=out, result=shape,
    )
    back1, back2 = sib(rest1), sib(rest2)

    far3, near3 = after([far3, near3], [out])
    across3 = by_near(far3)
    (sum3,) = products(
        table, t_rows, metas, [Group([quarter(1, near3), quarter(2, far3)], before=sum3)], [near3]
    )
    back3 = sib(sum3[1])

    out = place(table, out, other_columns[:2], [back1, back2], [sum3[0]])

    (across3,) = after([across3], [out])
    groups = [
        Group([quarter(3, across3)], before=[sum3[0]], column=columns[2]),
        Group([quarter(3, sib(across3))], before=[back3], column=other_columns[2]),
    ]
    ((out,), _) = products(table, [t_pp], [meta], groups, [], out=out, result=shape)
    return out


def on_device(t_pp, interaction, send_order, recv_order, ph_channel, recouple_weight):
    sent = functools.partial(meta_to_send, recv_order, ph_channel, recouple_weight)
    got = functools.partial(meta_of_rows, send_order)
    planes = lax.axis_size("chan") // 2
    if planes == 4 and lax.axis_size("int") == 4 and interaction.shape[0] == planes:
        return grid_plan(t_pp, interaction, sent, meta_over, got)
    return general_plan(t_pp, interaction, got(meta_over(sent())))


def solution(mesh):
    in_specs = (
        P(("chan", "int"), None),
        P(None, None, "int"),
        P(("chan", "int")),
        P(("chan", "int")),
        P("chan"),
        P("chan"),
    )
    out_specs = P(("chan", "int"), None)
    return jax.shard_map(
        on_device, mesh=mesh, in_specs=in_specs, out_specs=out_specs, check_vma=False
    )
```

```python
import functools

import jax
import jax.numpy as jnp
from jax import lax
from jax.experimental import pallas as pl
from jax.experimental.pallas import tpu as pltpu
from jax.sharding import PartitionSpec as P

VMEM_BYTES = 64 * 1024 * 1024 - 256 * 1024
IN_SMEM = pl.BlockSpec(memory_space=pltpu.SMEM)
IN_HBM = pl.BlockSpec(memory_space=pl.ANY)
PARAMS = pltpu.CompilerParams(vmem_limit_bytes=VMEM_BYTES)
NO_COST = pl.CostEstimate(flops=1, bytes_accessed=1, transcendentals=0)


def after(arrays, earlier):
    count = len(arrays)

    def body(*refs):
        del refs

    return pl.pallas_call(
        body,
        in_specs=[IN_HBM] * (count + len(earlier)),
        out_specs=[IN_HBM] * count,
        out_shape=[jax.ShapeDtypeStruct(x.shape, x.dtype) for x in arrays],
        input_output_aliases={n: n for n in range(count)},
        cost_estimate=NO_COST,
        compiler_params=PARAMS,
    )(*arrays, *earlier)


class Group:
    def __init__(self, blocks, before=None, column=None):
        self.blocks, self.before, self.column = blocks, before, column


def products_body(plan, scalars, *refs):
    layouts, places, finals, befores, sides, tile, stacked, in_count = plan
    hbm_rows = refs[: 2 * sides]
    place = 2 * sides
    array_count = sum(len(counts) for layout in layouts for counts in layout)
    if stacked:
        arrays = [refs[place].at[n] for n in range(array_count)]
        place += 1
    else:
        arrays = refs[place : place + array_count]
        place += array_count
    before_hbm = []
    for before in befores:
        before_hbm.append(refs[place : place + sides] if before else None)
        place += sides if before else 0
    outs = refs[in_count : in_count + sides * len(layouts)]
    scratch = refs[in_count + sides * len(layouts) :]
    t_refs, meta_refs = scratch[:sides], scratch[sides : 2 * sides]
    held = scratch[2 * sides : 2 * sides + array_count]
    staged, before_ref, t_sems, meta_sems, v_sems, before_sems, out_sems = scratch[2 * sides + array_count :]
    slots = t_refs[0].shape[0]
    width = staged.shape[2]
    tiles = slots // tile
    steps = [(side, i) for side in range(sides) for i in range(tiles)]

    def t_copy(step):
        side, i = steps[step]
        rows = pl.ds(i * tile, tile)
        return pltpu.make_async_copy(hbm_rows[side].at[rows, :], t_refs[side].at[rows, :], t_sems.at[step])

    def meta_copy(side):
        return pltpu.make_async_copy(hbm_rows[sides + side], meta_refs[side], meta_sems.at[side])

    def v_copy(n):
        return pltpu.make_async_copy(arrays[n], held[n], v_sems.at[n])

    def before_copy(g, side):
        rows = pl.ds(side * slots, slots)
        return pltpu.make_async_copy(before_hbm[g][side], before_ref.at[g, rows, :], before_sems.at[g * sides + side])

    def out_copy(g, step):
        side, i = steps[step]
        rows = pl.ds(i * tile, tile)
        if side == 0 and finals[g] is not None:
            first = next(n for n in range(len(finals)) if finals[n] is not None)
            columns = pl.ds(pl.multiple_of(scalars[finals[g]], 128), width)
            target = outs[first * sides].at[rows, columns]
        else:
            target = outs[g * sides + side].at[rows, :]
        return pltpu.make_async_copy(
            staged.at[g, pl.ds(step * tile, tile), :], target, out_sems.at[g * len(steps) + step]
        )

    v_copy(0).start()
    meta_copy(0).start()
    for step in range(tiles):
        t_copy(step).start()
    for n in range(1, array_count):
        v_copy(n).start()
    for step in range(tiles, len(steps)):
        t_copy(step).start()
    if sides == 2:
        meta_copy(1).start()
    for g in range(len(layouts)):
        for side in range(sides if befores[g] else 0):
            before_copy(g, side).start()
    for step, (side, i) in enumerate(steps):
        if i == 0:
            meta_copy(side).wait()
            for later in range(tiles):
                t_copy(step + later).wait()
            if step == 0:
                for n in range(array_count):
                    v_copy(n).wait()
            for g in range(len(layouts)):
                if befores[g]:
                    before_copy(g, side).wait()
        rows = pl.ds(i * tile, tile)
        here = pl.ds(step * tile, tile)
        used = 0
        for g, layout in enumerate(layouts):
            total = None
            for counts, (at, starts) in zip(layout, places[g]):
                channel = (jnp.int32(at) if stacked else scalars[at]).astype(jnp.float32)
                scale = jnp.where(meta_refs[side][rows, 0:1] == channel, meta_refs[side][rows, 1:2], 0.0)
                product = None
                for count, first in zip(counts, starts):
                    part = jnp.dot(
                        t_refs[side][rows, first : first + count],
                        held[used][...],
                        preferred_element_type=jnp.float32,
                    )
                    product = part if product is None else product + part
                    used += 1
                total = scale * product if total is None else total + scale * product
            if befores[g]:
                total = total + before_ref[g, here, :].astype(jnp.float32)
            staged[g, here, :] = total.astype(staged.dtype)
        if i == tiles - 1:
            for g in range(len(layouts)):
                for done in range(step - tiles + 1, step + 1):
                    out_copy(g, done).start()
    for g in range(len(layouts)):
        for step in range(len(steps)):
            out_copy(g, step).wait()


def products(table, t_rows, metas, groups, earlier, out=None, result=None):
    sides = len(t_rows)
    slots, depth = t_rows[0].shape
    dtype = t_rows[0].dtype
    tile = min(512, slots)
    stacked = not isinstance(groups[0].blocks[0][1], list)
    if stacked:
        arrays = [groups[0].blocks[0][1]]
        width = arrays[0].shape[2]
        held = [pltpu.VMEM(arrays[0].shape[1:], dtype)] * len(groups[0].blocks)
        layouts = (((depth,),) * len(groups[0].blocks),)
        places = (tuple((channel, (0,)) for channel, _ in groups[0].blocks),)
    else:
        arrays = [x for group in groups for _, parts in group.blocks for _, x in parts]
        width = arrays[0].shape[1]
        held = [pltpu.VMEM(x.shape, dtype) for x in arrays]
        layouts = tuple(
            tuple(tuple(x.shape[0] for _, x in parts) for _, parts in group.blocks) for group in groups
        )
        places = tuple(
            tuple((channel, tuple(n for n, _ in parts)) for channel, parts in group.blocks) for group in groups
        )
    operands = [*t_rows, *metas, *arrays]
    for group in groups:
        operands.extend(group.before or ())
    aliases, totals = {}, []
    for n, group in enumerate(groups):
        totals.extend([jax.ShapeDtypeStruct((slots, width), dtype)] * sides)
        if group.column is not None and result is not None:
            totals[n * sides] = jax.ShapeDtypeStruct(result, dtype)
            result = None
            if out is not None:
                aliases[1 + len(operands)] = n * sides
                operands.append(out)
        elif group.column is not None:
            totals[n * sides] = jax.ShapeDtypeStruct((16, width), dtype)
    operands.extend(earlier)
    steps = sides * (slots // tile)
    finals = tuple(group.column for group in groups)
    befores = tuple(group.before is not None for group in groups)
    plan = (layouts, places, finals, befores, sides, tile, stacked, len(operands))
    height = sides * slots
    sums = pl.pallas_call(
        functools.partial(products_body, plan),
        in_specs=[IN_SMEM] + [IN_HBM] * len(operands),
        out_specs=[IN_HBM] * len(totals),
        out_shape=totals,
        input_output_aliases=aliases,
        scratch_shapes=[
            *[pltpu.VMEM((slots, depth), dtype)] * sides,
            *[pltpu.VMEM(metas[0].shape, metas[0].dtype)] * sides,
            *held,
            pltpu.VMEM((len(groups), height, width), dtype),
            pltpu.VMEM((len(groups), height if any(befores) else 16, width), dtype),
            pltpu.SemaphoreType.DMA((steps,)),
            pltpu.SemaphoreType.DMA((sides,)),
            pltpu.SemaphoreType.DMA((len(held),)),
            pltpu.SemaphoreType.DMA((sides * len(groups),)),
            pltpu.SemaphoreType.DMA((steps * len(groups),)),
        ],
        cost_estimate=NO_COST,
        compiler_params=PARAMS,
    )(table, *operands)
    return [sums[n * sides : (n + 1) * sides] for n in range(len(groups))]


def place(table, out, columns, arrays, earlier):
    count, pieces = len(arrays), 2
    slots, width = arrays[0].shape
    part = slots // pieces

    def body(table_ref, *refs):
        out_ref, staged, got, put = refs[-4:]

        def fetch(n, p):
            rows = pl.ds(p * part, part)
            return pltpu.make_async_copy(refs[n].at[rows, :], staged.at[n, rows, :], got.at[n * pieces + p])

        def store(n, p):
            rows = pl.ds(p * part, part)
            there = pl.ds(pl.multiple_of(table_ref[columns[n]], 128), width)
            return pltpu.make_async_copy(staged.at[n, rows, :], out_ref.at[rows, there], put.at[n * pieces + p])

        every = [(n, p) for n in range(count) for p in range(pieces)]
        for n, p in every:
            fetch(n, p).start()
        for n, p in every:
            fetch(n, p).wait()
            store(n, p).start()
        for n, p in every:
            store(n, p).wait()

    return pl.pallas_call(
        body,
        in_specs=[IN_SMEM] + [IN_HBM] * (count + 1 + len(earlier)),
        out_specs=IN_HBM,
        out_shape=jax.ShapeDtypeStruct(out.shape, out.dtype),
        input_output_aliases={1 + count: 0},
        scratch_shapes=[
            pltpu.VMEM((count, slots, width), out.dtype),
            pltpu.SemaphoreType.DMA((count * pieces,)),
            pltpu.SemaphoreType.DMA((count * pieces,)),
        ],
        cost_estimate=NO_COST,
        compiler_params=PARAMS,
    )(table, *arrays, out, *earlier)


def inverse_take(order, values):
    hit = order[None, :] == jnp.arange(order.shape[0], dtype=order.dtype)[:, None]
    return [jnp.sum(jnp.where(hit, value[None, :], 0.0), axis=1) for value in values]


def meta_to_send(recv_order, ph_channel, recouple_weight, earlier=None):
    slots = recv_order.shape[0]
    group = lax.axis_size("chan")
    member = lax.axis_index("int") * slots
    ids = lax.dynamic_slice(ph_channel, (member,), (slots,)).astype(jnp.float32)
    scale = lax.dynamic_slice(recouple_weight, (member,), (slots,))
    back = jnp.stack(inverse_take(recv_order, [ids, scale]), axis=0)
    back = back.reshape(2, group, slots // group).transpose(1, 0, 2)
    return back if earlier is None else after([back], [earlier])[0]


def meta_over(back):
    return lax.all_to_all(back, "chan", split_axis=0, concat_axis=0, tiled=True)


def meta_of_rows(send_order, returned):
    back = returned.transpose(1, 0, 2).reshape(2, -1)
    ids, scale = inverse_take(send_order, [back[0], back[1]])
    lane = jnp.arange(128)[None, :]
    return jnp.where(lane == 0, ids[:, None], jnp.where(lane == 1, scale[:, None], 0.0))


def general_plan(t_pp, interaction, meta):
    slots, depth = t_pp.shape
    channels, _, width = interaction.shape
    group, members = lax.axis_size("chan"), lax.axis_size("int")
    flat = interaction.reshape(channels * depth, width)
    share = flat.shape[0] // group
    mine = lax.dynamic_slice(flat, (lax.axis_index("chan") * share, 0), (share, width))
    everyone = lax.all_gather(mine, ("chan", "int"), axis=0, tiled=False)
    everyone = everyone.reshape(group, members, share, width)
    out = None
    for member in range(members):
        whole = everyone[:, member].reshape(channels, depth, width)
        group_of = Group([(channel, whole) for channel in range(channels)], column=0)
        table = jnp.full((1,), member * width, jnp.int32)
        ((out,),) = products(table, [t_pp], [meta], [group_of], [], out=out, result=(slots, members * width))
    return out


def grid_plan(t_pp, interaction, meta_sent, meta_over, meta_got):
    slots, depth = t_pp.shape
    channels, _, width = interaction.shape
    group, members = lax.axis_size("chan"), lax.axis_size("int")
    axes = ("chan", "int")
    c, z = lax.axis_index("chan"), lax.axis_index("int")
    core, chip = c % 2, c // 2
    half, part = depth // 2, width // 2
    shape = (slots, members * width)

    def at(chan, member):
        return chan * members + member

    def along(pairs):
        return [(at(a, m), at(a, n)) for a in range(group) for m, n in pairs]

    outer = along([(0, 1), (1, 0), (2, 3), (3, 2)])
    middle = along([(1, 2), (2, 1)])
    outwards = along([(1, 0), (2, 3)])
    near_pairs = [(a, a ^ (4 if a % 2 else 2)) for a in range(group)]
    far_pairs = [(a, a ^ (2 if a % 2 else 4)) for a in range(group)]
    other = [(a, a ^ 1) for a in range(group)]

    def step(x, pairs):
        return lax.ppermute(x, axes, pairs)

    def by_near(x):
        return lax.ppermute(x, "chan", near_pairs)

    def by_far(x):
        return lax.ppermute(x, "chan", far_pairs)

    def sib(x):
        return lax.ppermute(x, "chan", other)

    end = (z == 0) | (z == members - 1)
    low = z < members // 2
    mine, theirs = core * part, (1 - core) * part
    starts = [(z ^ 1) * width, jnp.where(low, 2, 1) * width, jnp.where(low, 3, 0) * width]
    table = [chip, chip ^ (1 + core), chip ^ (2 - core), chip ^ 3] + [z * width] + [n + mine for n in starts] + [n + theirs for n in starts]
    table = jnp.stack(table).astype(jnp.int32)
    own_column, columns, other_columns = 4, (5, 6, 7), (8, 9, 10)

    def quarter(n, x):
        return (n, [(0, x)])

    def own_rows(channel):
        rows = lax.dynamic_slice(interaction, (channel, 0, core * part), (1, depth, part))
        return rows.reshape(depth, part)

    (own,) = after([own_rows(chip)], [])
    p1, p2 = step(own, outer), step(own, middle)
    other_t = sib(t_pp)
    fence = sib(own[:16])
    meta = meta_got(meta_over(meta_sent(fence)))
    (later,) = after([table], [meta])
    extra = own_rows(later[3])
    meta, extra = after([meta, extra], [own])

    p1, p2, other_t = after([p1, p2, other_t], [meta])
    p3, near1, far1, p4 = step(p2, outwards), by_near(p1), by_far(p1), step(p1, middle)
    other_meta = sib(meta)
    local = Group([(channel, interaction) for channel in range(channels)], column=own_column)
    ((out,),) = products(table, [t_pp], [meta], [local], [p1], result=shape)

    (near1,) = after([near1], [out])
    (p3,) = after([p3], [near1])
    far1, other_meta = after([far1, other_meta], [p3])
    (p4,) = after([p4], [far1])
    p5 = step(p4, outwards)
    s2 = jnp.where(end, p3, p2)
    far2, near2 = by_far(s2), by_near(s2)
    t_rows = [t_pp, other_t]
    metas = [meta, other_meta]
    (sum1,) = products(table, t_rows, metas, [Group([quarter(0, p1), quarter(1, near1), quarter(2, far1)])], [s2])

    (p5,) = after([p5], [sum1[0]])
    (extra,) = after([extra], [p5])
    e = step(extra, outer)
    far2, near2 = after([far2, near2], [extra])
    across2 = by_near(far2)
    s3 = jnp.where(end, p5, p4)
    far3, near3 = by_far(s3), by_near(s3)
    sum2, sum3 = products(
        table, t_rows, metas,
        [Group([quarter(0, s2), quarter(1, near2), quarter(2, far2)]), Group([quarter(0, s3)])],
        [s3],
    )
    e, across2 = after([e, across2], [sum2[0]])
    (out, rest1), (_, rest2) = products(
        table, t_rows, metas,
        [
            Group([quarter(3, e)], before=sum1, column=columns[0]),
            Group([quarter(3, across2)], before=sum2, column=columns[1]),
        ],
        [across2], out=out, result=shape,
    )
    back1, back2 = sib(rest1), sib(rest2)

    far3, near3 = after([far3, near3], [out])
    across3 = by_near(far3)
    (sum3,) = products(
        table, t_rows, metas, [Group([quarter(1, near3), quarter(2, far3)], before=sum3)], [near3]
    )
    back3 = sib(sum3[1])
    out = place(table, out, other_columns[:2], [back1, back2], [sum3[0]])

    (across3,) = after([across3], [out])
    groups = [
        Group([quarter(3, across3)], before=[sum3[0]], column=columns[2]),
        Group([quarter(3, sib(across3))], before=[back3], column=other_columns[2]),
    ]
    ((out,), _) = products(table, [t_pp], [meta], groups, [], out=out, result=shape)
    return out


def on_device(t_pp, interaction, send_order, recv_order, ph_channel, recouple_weight):
    sent = functools.partial(meta_to_send, recv_order, ph_channel, recouple_weight)
    got = functools.partial(meta_of_rows, send_order)
    planes = lax.axis_size("chan") // 2
    if planes == 4 and lax.axis_size("int") == 4 and interaction.shape[0] == planes:
        return grid_plan(t_pp, interaction, sent, meta_over, got)
    return general_plan(t_pp, interaction, got(meta_over(sent())))


def solution(mesh):
    in_specs = (
        P(("chan", "int"), None),
        P(None, None, "int"),
        P(("chan", "int")),
        P(("chan", "int")),
        P("chan"),
        P("chan"),
    )
    out_specs = P(("chan", "int"), None)
    return jax.shard_map(
        on_device, mesh=mesh, in_specs=in_specs, out_specs=out_specs, check_vma=False
    )
```

```python
import functools

import jax
import jax.numpy as jnp
from jax import lax
from jax.experimental import pallas as pl
from jax.experimental.pallas import tpu as pltpu
from jax.sharding import PartitionSpec as P

VMEM_BYTES = 64 * 1024 * 1024 - 256 * 1024
IN_SMEM = pl.BlockSpec(memory_space=pltpu.SMEM)
IN_HBM = pl.BlockSpec(memory_space=pl.ANY)
PARAMS = pltpu.CompilerParams(vmem_limit_bytes=VMEM_BYTES)
NO_COST = pl.CostEstimate(flops=1, bytes_accessed=1, transcendentals=0)


def after(arrays, earlier):
    count = len(arrays)

    def body(*refs):
        del refs

    return pl.pallas_call(
        body,
        in_specs=[IN_HBM] * (count + len(earlier)),
        out_specs=[IN_HBM] * count,
        out_shape=[jax.ShapeDtypeStruct(x.shape, x.dtype) for x in arrays],
        input_output_aliases={n: n for n in range(count)},
        cost_estimate=NO_COST,
        compiler_params=PARAMS,
    )(*arrays, *earlier)


class Group:
    def __init__(self, blocks, before=None, column=None):
        self.blocks, self.before, self.column = blocks, before, column


def products_body(plan, scalars, *refs):
    layouts, places, finals, befores, sides, tile, stacked, in_count = plan
    hbm_rows = refs[: 2 * sides]
    place = 2 * sides
    array_count = sum(len(counts) for layout in layouts for counts in layout)
    if stacked:
        arrays = [refs[place].at[n] for n in range(array_count)]
        place += 1
    else:
        arrays = refs[place : place + array_count]
        place += array_count
    before_hbm = []
    for before in befores:
        before_hbm.append(refs[place : place + sides] if before else None)
        place += sides if before else 0
    outs = refs[in_count : in_count + sides * len(layouts)]
    scratch = refs[in_count + sides * len(layouts) :]
    t_refs, meta_refs = scratch[:sides], scratch[sides : 2 * sides]
    held = scratch[2 * sides : 2 * sides + array_count]
    staged, before_ref, t_sems, meta_sems, v_sems, before_sems, out_sems = scratch[2 * sides + array_count :]
    slots = t_refs[0].shape[0]
    width = staged.shape[2]
    tiles = slots // tile
    steps = [(side, i) for side in range(sides) for i in range(tiles)]

    def t_copy(step):
        side, i = steps[step]
        rows = pl.ds(i * tile, tile)
        return pltpu.make_async_copy(hbm_rows[side].at[rows, :], t_refs[side].at[rows, :], t_sems.at[step])

    def meta_copy(side):
        return pltpu.make_async_copy(hbm_rows[sides + side], meta_refs[side], meta_sems.at[side])

    def v_copy(n):
        return pltpu.make_async_copy(arrays[n], held[n], v_sems.at[n])

    def before_copy(g, side):
        rows = pl.ds(side * slots, slots)
        return pltpu.make_async_copy(before_hbm[g][side], before_ref.at[g, rows, :], before_sems.at[g * sides + side])

    def out_copy(g, step):
        side, i = steps[step]
        rows = pl.ds(i * tile, tile)
        if side == 0 and finals[g] is not None:
            first = next(n for n in range(len(finals)) if finals[n] is not None)
            columns = pl.ds(pl.multiple_of(scalars[finals[g]], 128), width)
            target = outs[first * sides].at[rows, columns]
        else:
            target = outs[g * sides + side].at[rows, :]
        return pltpu.make_async_copy(
            staged.at[g, pl.ds(step * tile, tile), :], target, out_sems.at[g * len(steps) + step]
        )

    v_copy(0).start()
    meta_copy(0).start()
    for step in range(tiles):
        t_copy(step).start()
    for n in range(1, array_count):
        v_copy(n).start()
    for step in range(tiles, len(steps)):
        t_copy(step).start()
    if sides == 2:
        meta_copy(1).start()
    for g in range(len(layouts)):
        for side in range(sides if befores[g] else 0):
            before_copy(g, side).start()
    for step, (side, i) in enumerate(steps):
        if i == 0:
            meta_copy(side).wait()
            for later in range(tiles):
                t_copy(step + later).wait()
            if step == 0:
                for n in range(array_count):
                    v_copy(n).wait()
            for g in range(len(layouts)):
                if befores[g]:
                    before_copy(g, side).wait()
        rows = pl.ds(i * tile, tile)
        here = pl.ds(step * tile, tile)
        used = 0
        for g, layout in enumerate(layouts):
            total = None
            for counts, (at, starts) in zip(layout, places[g]):
                channel = (jnp.int32(at) if stacked else scalars[at]).astype(jnp.float32)
                scale = jnp.where(meta_refs[side][rows, 0:1] == channel, meta_refs[side][rows, 1:2], 0.0)
                product = None
                for count, first in zip(counts, starts):
                    part = jnp.dot(
                        t_refs[side][rows, first : first + count],
                        held[used][...],
                        preferred_element_type=jnp.float32,
                    )
                    product = part if product is None else product + part
                    used += 1
                total = scale * product if total is None else total + scale * product
            if befores[g]:
                total = total + before_ref[g, here, :].astype(jnp.float32)
            staged[g, here, :] = total.astype(staged.dtype)
        if i == tiles - 1:
            for g in range(len(layouts)):
                for done in range(step - tiles + 1, step + 1):
                    out_copy(g, done).start()
    for g in range(len(layouts)):
        for step in range(len(steps)):
            out_copy(g, step).wait()


def products(table, t_rows, metas, groups, earlier, out=None, result=None):
    sides = len(t_rows)
    slots, depth = t_rows[0].shape
    dtype = t_rows[0].dtype
    tile = min(512, slots)
    stacked = not isinstance(groups[0].blocks[0][1], list)
    if stacked:
        arrays = [groups[0].blocks[0][1]]
        width = arrays[0].shape[2]
        held = [pltpu.VMEM(arrays[0].shape[1:], dtype)] * len(groups[0].blocks)
        layouts = (((depth,),) * len(groups[0].blocks),)
        places = (tuple((channel, (0,)) for channel, _ in groups[0].blocks),)
    else:
        arrays = [x for group in groups for _, parts in group.blocks for _, x in parts]
        width = arrays[0].shape[1]
        held = [pltpu.VMEM(x.shape, dtype) for x in arrays]
        layouts = tuple(
            tuple(tuple(x.shape[0] for _, x in parts) for _, parts in group.blocks) for group in groups
        )
        places = tuple(
            tuple((channel, tuple(n for n, _ in parts)) for channel, parts in group.blocks) for group in groups
        )
    operands = [*t_rows, *metas, *arrays]
    for group in groups:
        operands.extend(group.before or ())
    aliases, totals = {}, []
    for n, group in enumerate(groups):
        totals.extend([jax.ShapeDtypeStruct((slots, width), dtype)] * sides)
        if group.column is not None and result is not None:
            totals[n * sides] = jax.ShapeDtypeStruct(result, dtype)
            result = None
            if out is not None:
                aliases[1 + len(operands)] = n * sides
                operands.append(out)
        elif group.column is not None:
            totals[n * sides] = jax.ShapeDtypeStruct((16, width), dtype)
    operands.extend(earlier)
    steps = sides * (slots // tile)
    finals = tuple(group.column for group in groups)
    befores = tuple(group.before is not None for group in groups)
    plan = (layouts, places, finals, befores, sides, tile, stacked, len(operands))
    height = sides * slots
    sums = pl.pallas_call(
        functools.partial(products_body, plan),
        in_specs=[IN_SMEM] + [IN_HBM] * len(operands),
        out_specs=[IN_HBM] * len(totals),
        out_shape=totals,
        input_output_aliases=aliases,
        scratch_shapes=[
            *[pltpu.VMEM((slots, depth), dtype)] * sides,
            *[pltpu.VMEM(metas[0].shape, metas[0].dtype)] * sides,
            *held,
            pltpu.VMEM((len(groups), height, width), dtype),
            pltpu.VMEM((len(groups), height if any(befores) else 16, width), dtype),
            pltpu.SemaphoreType.DMA((steps,)),
            pltpu.SemaphoreType.DMA((sides,)),
            pltpu.SemaphoreType.DMA((len(held),)),
            pltpu.SemaphoreType.DMA((sides * len(groups),)),
            pltpu.SemaphoreType.DMA((steps * len(groups),)),
        ],
        cost_estimate=NO_COST,
        compiler_params=PARAMS,
    )(table, *operands)
    return [sums[n * sides : (n + 1) * sides] for n in range(len(groups))]


def place(table, out, columns, arrays, earlier):
    count, pieces = len(arrays), 2
    slots, width = arrays[0].shape
    part = slots // pieces

    def body(table_ref, *refs):
        out_ref, staged, got, put = refs[-4:]

        def fetch(n, p):
            rows = pl.ds(p * part, part)
            return pltpu.make_async_copy(refs[n].at[rows, :], staged.at[n, rows, :], got.at[n * pieces + p])

        def store(n, p):
            rows = pl.ds(p * part, part)
            there = pl.ds(pl.multiple_of(table_ref[columns[n]], 128), width)
            return pltpu.make_async_copy(staged.at[n, rows, :], out_ref.at[rows, there], put.at[n * pieces + p])

        every = [(n, p) for n in range(count) for p in range(pieces)]
        for n, p in every:
            fetch(n, p).start()
        for n, p in every:
            fetch(n, p).wait()
            store(n, p).start()
        for n, p in every:
            store(n, p).wait()

    return pl.pallas_call(
        body,
        in_specs=[IN_SMEM] + [IN_HBM] * (count + 1 + len(earlier)),
        out_specs=IN_HBM,
        out_shape=jax.ShapeDtypeStruct(out.shape, out.dtype),
        input_output_aliases={1 + count: 0},
        scratch_shapes=[
            pltpu.VMEM((count, slots, width), out.dtype),
            pltpu.SemaphoreType.DMA((count * pieces,)),
            pltpu.SemaphoreType.DMA((count * pieces,)),
        ],
        cost_estimate=NO_COST,
        compiler_params=PARAMS,
    )(table, *arrays, out, *earlier)


def inverse_take(order, values):
    hit = order[None, :] == jnp.arange(order.shape[0], dtype=order.dtype)[:, None]
    return [jnp.sum(jnp.where(hit, value[None, :], 0.0), axis=1) for value in values]


def meta_to_send(recv_order, ph_channel, recouple_weight, earlier=None):
    slots = recv_order.shape[0]
    group = lax.axis_size("chan")
    member = lax.axis_index("int") * slots
    ids = lax.dynamic_slice(ph_channel, (member,), (slots,)).astype(jnp.float32)
    scale = lax.dynamic_slice(recouple_weight, (member,), (slots,))
    back = jnp.stack(inverse_take(recv_order, [ids, scale]), axis=0)
    back = back.reshape(2, group, slots // group).transpose(1, 0, 2)
    return back if earlier is None else after([back], [earlier])[0]


def meta_over(back):
    return lax.all_to_all(back, "chan", split_axis=0, concat_axis=0, tiled=True)


def meta_of_rows(send_order, returned):
    back = returned.transpose(1, 0, 2).reshape(2, -1)
    ids, scale = inverse_take(send_order, [back[0], back[1]])
    lane = jnp.arange(128)[None, :]
    return jnp.where(lane == 0, ids[:, None], jnp.where(lane == 1, scale[:, None], 0.0))


def general_plan(t_pp, interaction, meta):
    slots, depth = t_pp.shape
    channels, _, width = interaction.shape
    group, members = lax.axis_size("chan"), lax.axis_size("int")
    flat = interaction.reshape(channels * depth, width)
    share = flat.shape[0] // group
    mine = lax.dynamic_slice(flat, (lax.axis_index("chan") * share, 0), (share, width))
    everyone = lax.all_gather(mine, ("chan", "int"), axis=0, tiled=False)
    everyone = everyone.reshape(group, members, share, width)
    out = None
    for member in range(members):
        whole = everyone[:, member].reshape(channels, depth, width)
        group_of = Group([(channel, whole) for channel in range(channels)], column=0)
        table = jnp.full((1,), member * width, jnp.int32)
        ((out,),) = products(table, [t_pp], [meta], [group_of], [], out=out, result=(slots, members * width))
    return out


def grid_plan(t_pp, interaction, meta_sent, meta_over, meta_got):
    slots, depth = t_pp.shape
    channels, _, width = interaction.shape
    group, members = lax.axis_size("chan"), lax.axis_size("int")
    axes = ("chan", "int")
    c, z = lax.axis_index("chan"), lax.axis_index("int")
    core, chip = c % 2, c // 2
    half, part = depth // 2, width // 2
    shape = (slots, members * width)

    def at(chan, member):
        return chan * members + member

    def along(pairs):
        return [(at(a, m), at(a, n)) for a in range(group) for m, n in pairs]

    outer = along([(0, 1), (1, 0), (2, 3), (3, 2)])
    middle = along([(1, 2), (2, 1)])
    outwards = along([(1, 0), (2, 3)])
    near_pairs = [(a, a ^ (4 if a % 2 else 2)) for a in range(group)]
    far_pairs = [(a, a ^ (2 if a % 2 else 4)) for a in range(group)]
    other = [(a, a ^ 1) for a in range(group)]

    def step(x, pairs):
        return lax.ppermute(x, axes, pairs)

    def by_near(x):
        return lax.ppermute(x, "chan", near_pairs)

    def by_far(x):
        return lax.ppermute(x, "chan", far_pairs)

    def sib(x):
        return lax.ppermute(x, "chan", other)

    end = (z == 0) | (z == members - 1)
    low = z < members // 2
    mine, theirs = core * part, (1 - core) * part
    starts = [(z ^ 1) * width, jnp.where(low, 2, 1) * width, jnp.where(low, 3, 0) * width]
    table = [chip, chip ^ (1 + core), chip ^ (2 - core), chip ^ 3] + [z * width] + [n + mine for n in starts] + [n + theirs for n in starts]
    table = jnp.stack(table).astype(jnp.int32)
    own_column, columns, other_columns = 4, (5, 6, 7), (8, 9, 10)

    def quarter(n, x):
        return (n, [(0, x)])

    def own_rows(channel):
        rows = lax.dynamic_slice(interaction, (channel, 0, core * part), (1, depth, part))
        return rows.reshape(depth, part)

    (own,) = after([own_rows(chip)], [])
    p1, p2 = step(own, outer), step(own, middle)
    other_t = sib(t_pp)
    fence = sib(own[:16])
    meta = meta_got(meta_over(meta_sent(fence)))
    (later,) = after([table], [meta])
    extra = own_rows(later[3])
    meta, extra = after([meta, extra], [own])

    (p1,) = after([p1], [meta])
    p2, other_t = after([p2, other_t], [p1])
    p3, near1, far1, p4 = step(p2, outwards), by_near(p1), by_far(p1), step(p1, middle)
    other_meta = sib(meta)
    local = Group([(channel, interaction) for channel in range(channels)], column=own_column)
    ((out,),) = products(table, [t_pp], [meta], [local], [p1], result=shape)

    (near1,) = after([near1], [out])
    far1, other_meta = after([far1, other_meta], [near1])
    (p3,) = after([p3], [far1])
    s2 = jnp.where(end, p3, p2)
    far2, near2 = by_far(s2), by_near(s2)
    (p4,) = after([p4], [s2])
    p5 = step(p4, outwards)
    t_rows = [t_pp, other_t]
    metas = [meta, other_meta]
    (sum1,) = products(table, t_rows, metas, [Group([quarter(0, p1), quarter(1, near1), quarter(2, far1)])], [p4])

    far2, near2 = after([far2, near2], [sum1[0]])
    across2 = by_near(far2)
    (p5,) = after([p5], [far2])
    (extra,) = after([extra], [p5])
    e = step(extra, outer)
    s3 = jnp.where(end, p5, p4)
    far3, near3 = by_far(s3), by_near(s3)
    sum2, sum3 = products(
        table, t_rows, metas,
        [Group([quarter(0, s2), quarter(1, near2), quarter(2, far2)]), Group([quarter(0, s3)])],
        [s3],
    )
    e, across2 = after([e, across2], [sum2[0]])
    (out, rest1), (_, rest2) = products(
        table, t_rows, metas,
        [
            Group([quarter(3, e)], before=sum1, column=columns[0]),
            Group([quarter(3, across2)], before=sum2, column=columns[1]),
        ],
        [across2], out=out, result=shape,
    )
    back1, back2 = sib(rest1), sib(rest2)

    far3, near3 = after([far3, near3], [out])
    across3 = by_near(far3)
    (sum3,) = products(
        table, t_rows, metas, [Group([quarter(1, near3), quarter(2, far3)], before=sum3)], [near3]
    )
    back3 = sib(sum3[1])
    out = place(table, out, other_columns[:2], [back1, back2], [sum3[0]])

    (across3,) = after([across3], [out])
    groups = [
        Group([quarter(3, across3)], before=[sum3[0]], column=columns[2]),
        Group([quarter(3, sib(across3))], before=[back3], column=other_columns[2]),
    ]
    ((out,), _) = products(table, [t_pp], [meta], groups, [], out=out, result=shape)
    return out


def on_device(t_pp, interaction, send_order, recv_order, ph_channel, recouple_weight):
    sent = functools.partial(meta_to_send, recv_order, ph_channel, recouple_weight)
    got = functools.partial(meta_of_rows, send_order)
    planes = lax.axis_size("chan") // 2
    if planes == 4 and lax.axis_size("int") == 4 and interaction.shape[0] == planes:
        return grid_plan(t_pp, interaction, sent, meta_over, got)
    return general_plan(t_pp, interaction, got(meta_over(sent())))


def solution(mesh):
    in_specs = (
        P(("chan", "int"), None),
        P(None, None, "int"),
        P(("chan", "int")),
        P(("chan", "int")),
        P("chan"),
        P("chan"),
    )
    out_specs = P(("chan", "int"), None)
    return jax.shard_map(
        on_device, mesh=mesh, in_specs=in_specs, out_specs=out_specs, check_vma=False
    )
```

```python
import functools

import jax
import jax.numpy as jnp
from jax import lax
from jax.experimental import pallas as pl
from jax.experimental.pallas import tpu as pltpu
from jax.sharding import PartitionSpec as P

VMEM_BYTES = 64 * 1024 * 1024 - 256 * 1024
IN_SMEM = pl.BlockSpec(memory_space=pltpu.SMEM)
IN_HBM = pl.BlockSpec(memory_space=pl.ANY)
PARAMS = pltpu.CompilerParams(vmem_limit_bytes=VMEM_BYTES)
NO_COST = pl.CostEstimate(flops=1, bytes_accessed=1, transcendentals=0)


def after(arrays, earlier):
    count = len(arrays)

    def body(*refs):
        del refs

    return pl.pallas_call(
        body,
        in_specs=[IN_HBM] * (count + len(earlier)),
        out_specs=[IN_HBM] * count,
        out_shape=[jax.ShapeDtypeStruct(x.shape, x.dtype) for x in arrays],
        input_output_aliases={n: n for n in range(count)},
        cost_estimate=NO_COST,
        compiler_params=PARAMS,
    )(*arrays, *earlier)


class Group:
    def __init__(self, blocks, before=None, column=None):
        self.blocks, self.before, self.column = blocks, before, column


def products_body(plan, scalars, *refs):
    layouts, places, finals, befores, sides, tile, stacked, in_count = plan
    hbm_rows = refs[: 2 * sides]
    place = 2 * sides
    array_count = sum(len(counts) for layout in layouts for counts in layout)
    if stacked:
        arrays = [refs[place].at[n] for n in range(array_count)]
        place += 1
    else:
        arrays = refs[place : place + array_count]
        place += array_count
    before_hbm = []
    for before in befores:
        before_hbm.append(refs[place : place + sides] if before else None)
        place += sides if before else 0
    outs = refs[in_count : in_count + sides * len(layouts)]
    scratch = refs[in_count + sides * len(layouts) :]
    t_refs, meta_refs = scratch[:sides], scratch[sides : 2 * sides]
    held = scratch[2 * sides : 2 * sides + array_count]
    staged, before_ref, t_sems, meta_sems, v_sems, before_sems, out_sems = scratch[2 * sides + array_count :]
    slots = t_refs[0].shape[0]
    width = staged.shape[2]
    tiles = slots // tile
    steps = [(side, i) for side in range(sides) for i in range(tiles)]

    def t_copy(step):
        side, i = steps[step]
        rows = pl.ds(i * tile, tile)
        return pltpu.make_async_copy(hbm_rows[side].at[rows, :], t_refs[side].at[rows, :], t_sems.at[step])

    def meta_copy(side):
        return pltpu.make_async_copy(hbm_rows[sides + side], meta_refs[side], meta_sems.at[side])

    def v_copy(n):
        return pltpu.make_async_copy(arrays[n], held[n], v_sems.at[n])

    def before_copy(g, side):
        rows = pl.ds(side * slots, slots)
        return pltpu.make_async_copy(before_hbm[g][side], before_ref.at[g, rows, :], before_sems.at[g * sides + side])

    def out_copy(g, step):
        side, i = steps[step]
        rows = pl.ds(i * tile, tile)
        if side == 0 and finals[g] is not None:
            first = next(n for n in range(len(finals)) if finals[n] is not None)
            columns = pl.ds(pl.multiple_of(scalars[finals[g]], 128), width)
            target = outs[first * sides].at[rows, columns]
        else:
            target = outs[g * sides + side].at[rows, :]
        return pltpu.make_async_copy(
            staged.at[g, pl.ds(step * tile, tile), :], target, out_sems.at[g * len(steps) + step]
        )

    v_copy(0).start()
    meta_copy(0).start()
    for step in range(tiles):
        t_copy(step).start()
    for n in range(1, array_count):
        v_copy(n).start()
    for step in range(tiles, len(steps)):
        t_copy(step).start()
    if sides == 2:
        meta_copy(1).start()
    for g in range(len(layouts)):
        for side in range(sides if befores[g] else 0):
            before_copy(g, side).start()
    for step, (side, i) in enumerate(steps):
        if i == 0:
            meta_copy(side).wait()
            for later in range(tiles):
                t_copy(step + later).wait()
            if step == 0:
                for n in range(array_count):
                    v_copy(n).wait()
            for g in range(len(layouts)):
                if befores[g]:
                    before_copy(g, side).wait()
        rows = pl.ds(i * tile, tile)
        here = pl.ds(step * tile, tile)
        used = 0
        for g, layout in enumerate(layouts):
            total = None
            for counts, (at, starts) in zip(layout, places[g]):
                channel = (jnp.int32(at) if stacked else scalars[at]).astype(jnp.float32)
                scale = jnp.where(meta_refs[side][rows, 0:1] == channel, meta_refs[side][rows, 1:2], 0.0)
                product = None
                for count, first in zip(counts, starts):
                    part = jnp.dot(
                        t_refs[side][rows, first : first + count],
                        held[used][...],
                        preferred_element_type=jnp.float32,
                    )
                    product = part if product is None else product + part
                    used += 1
                total = scale * product if total is None else total + scale * product
            if total is None:
                staged[g, here, :] = before_ref[g, here, :]
                continue
            if befores[g]:
                total = total + before_ref[g, here, :].astype(jnp.float32)
            staged[g, here, :] = total.astype(staged.dtype)
        if i == tiles - 1:
            for g in range(len(layouts)):
                for done in range(step - tiles + 1, step + 1):
                    out_copy(g, done).start()
    for g in range(len(layouts)):
        for step in range(len(steps)):
            out_copy(g, step).wait()


def products(table, t_rows, metas, groups, earlier, out=None, result=None):
    sides = len(t_rows)
    slots, depth = t_rows[0].shape
    dtype = t_rows[0].dtype
    tile = min(512, slots)
    stacked = not isinstance(groups[0].blocks[0][1], list)
    if stacked:
        arrays = [groups[0].blocks[0][1]]
        width = arrays[0].shape[2]
        held = [pltpu.VMEM(arrays[0].shape[1:], dtype)] * len(groups[0].blocks)
        layouts = (((depth,),) * len(groups[0].blocks),)
        places = (tuple((channel, (0,)) for channel, _ in groups[0].blocks),)
    else:
        arrays = [x for group in groups for _, parts in group.blocks for _, x in parts]
        width = arrays[0].shape[1]
        held = [pltpu.VMEM(x.shape, dtype) for x in arrays]
        layouts = tuple(
            tuple(tuple(x.shape[0] for _, x in parts) for _, parts in group.blocks) for group in groups
        )
        places = tuple(
            tuple((channel, tuple(n for n, _ in parts)) for channel, parts in group.blocks) for group in groups
        )
    operands = [*t_rows, *metas, *arrays]
    for group in groups:
        operands.extend(group.before or ())
    aliases, totals = {}, []
    for n, group in enumerate(groups):
        totals.extend([jax.ShapeDtypeStruct((slots, width), dtype)] * sides)
        if group.column is not None and result is not None:
            totals[n * sides] = jax.ShapeDtypeStruct(result, dtype)
            result = None
            if out is not None:
                aliases[1 + len(operands)] = n * sides
                operands.append(out)
        elif group.column is not None:
            totals[n * sides] = jax.ShapeDtypeStruct((16, width), dtype)
    operands.extend(earlier)
    steps = sides * (slots // tile)
    finals = tuple(group.column for group in groups)
    befores = tuple(group.before is not None for group in groups)
    plan = (layouts, places, finals, befores, sides, tile, stacked, len(operands))
    height = sides * slots
    sums = pl.pallas_call(
        functools.partial(products_body, plan),
        in_specs=[IN_SMEM] + [IN_HBM] * len(operands),
        out_specs=[IN_HBM] * len(totals),
        out_shape=totals,
        input_output_aliases=aliases,
        scratch_shapes=[
            *[pltpu.VMEM((slots, depth), dtype)] * sides,
            *[pltpu.VMEM(metas[0].shape, metas[0].dtype)] * sides,
            *held,
            pltpu.VMEM((len(groups), height, width), dtype),
            pltpu.VMEM((len(groups), height if any(befores) else 16, width), dtype),
            pltpu.SemaphoreType.DMA((steps,)),
            pltpu.SemaphoreType.DMA((sides,)),
            pltpu.SemaphoreType.DMA((len(held),)),
            pltpu.SemaphoreType.DMA((sides * len(groups),)),
            pltpu.SemaphoreType.DMA((steps * len(groups),)),
        ],
        cost_estimate=NO_COST,
        compiler_params=PARAMS,
    )(table, *operands)
    return [sums[n * sides : (n + 1) * sides] for n in range(len(groups))]


def place(table, out, columns, arrays, earlier):
    count, pieces = len(arrays), 2
    slots, width = arrays[0].shape
    part = slots // pieces

    def body(table_ref, *refs):
        out_ref, staged, got, put = refs[-4:]

        def fetch(n, p):
            rows = pl.ds(p * part, part)
            return pltpu.make_async_copy(refs[n].at[rows, :], staged.at[n, rows, :], got.at[n * pieces + p])

        def store(n, p):
            rows = pl.ds(p * part, part)
            there = pl.ds(pl.multiple_of(table_ref[columns[n]], 128), width)
            return pltpu.make_async_copy(staged.at[n, rows, :], out_ref.at[rows, there], put.at[n * pieces + p])

        every = [(n, p) for n in range(count) for p in range(pieces)]
        for n, p in every:
            fetch(n, p).start()
        for n, p in every:
            fetch(n, p).wait()
            store(n, p).start()
        for n, p in every:
            store(n, p).wait()

    return pl.pallas_call(
        body,
        in_specs=[IN_SMEM] + [IN_HBM] * (count + 1 + len(earlier)),
        out_specs=IN_HBM,
        out_shape=jax.ShapeDtypeStruct(out.shape, out.dtype),
        input_output_aliases={1 + count: 0},
        scratch_shapes=[
            pltpu.VMEM((count, slots, width), out.dtype),
            pltpu.SemaphoreType.DMA((count * pieces,)),
            pltpu.SemaphoreType.DMA((count * pieces,)),
        ],
        cost_estimate=NO_COST,
        compiler_params=PARAMS,
    )(table, *arrays, out, *earlier)


def inverse_take(order, values):
    hit = order[None, :] == jnp.arange(order.shape[0], dtype=order.dtype)[:, None]
    return [jnp.sum(jnp.where(hit, value[None, :], 0.0), axis=1) for value in values]


def meta_to_send(recv_order, ph_channel, recouple_weight, earlier=None):
    slots = recv_order.shape[0]
    group = lax.axis_size("chan")
    member = lax.axis_index("int") * slots
    ids = lax.dynamic_slice(ph_channel, (member,), (slots,)).astype(jnp.float32)
    scale = lax.dynamic_slice(recouple_weight, (member,), (slots,))
    back = jnp.stack(inverse_take(recv_order, [ids, scale]), axis=0)
    back = back.reshape(2, group, slots // group).transpose(1, 0, 2)
    return back if earlier is None else after([back], [earlier])[0]


def meta_over(back):
    return lax.all_to_all(back, "chan", split_axis=0, concat_axis=0, tiled=True)


def meta_of_rows(send_order, returned):
    back = returned.transpose(1, 0, 2).reshape(2, -1)
    ids, scale = inverse_take(send_order, [back[0], back[1]])
    lane = jnp.arange(128)[None, :]
    return jnp.where(lane == 0, ids[:, None], jnp.where(lane == 1, scale[:, None], 0.0))


def general_plan(t_pp, interaction, meta):
    slots, depth = t_pp.shape
    channels, _, width = interaction.shape
    group, members = lax.axis_size("chan"), lax.axis_size("int")
    flat = interaction.reshape(channels * depth, width)
    share = flat.shape[0] // group
    mine = lax.dynamic_slice(flat, (lax.axis_index("chan") * share, 0), (share, width))
    everyone = lax.all_gather(mine, ("chan", "int"), axis=0, tiled=False)
    everyone = everyone.reshape(group, members, share, width)
    out = None
    for member in range(members):
        whole = everyone[:, member].reshape(channels, depth, width)
        group_of = Group([(channel, whole) for channel in range(channels)], column=0)
        table = jnp.full((1,), member * width, jnp.int32)
        ((out,),) = products(table, [t_pp], [meta], [group_of], [], out=out, result=(slots, members * width))
    return out


def grid_plan(t_pp, interaction, meta_sent, meta_over, meta_got):
    slots, depth = t_pp.shape
    channels, _, width = interaction.shape
    group, members = lax.axis_size("chan"), lax.axis_size("int")
    axes = ("chan", "int")
    c, z = lax.axis_index("chan"), lax.axis_index("int")
    core, chip = c % 2, c // 2
    half, part = depth // 2, width // 2
    shape = (slots, members * width)

    def at(chan, member):
        return chan * members + member

    def along(pairs):
        return [(at(a, m), at(a, n)) for a in range(group) for m, n in pairs]

    outer = along([(0, 1), (1, 0), (2, 3), (3, 2)])
    middle = along([(1, 2), (2, 1)])
    outwards = along([(1, 0), (2, 3)])
    near_pairs = [(a, a ^ (4 if a % 2 else 2)) for a in range(group)]
    far_pairs = [(a, a ^ (2 if a % 2 else 4)) for a in range(group)]
    other = [(a, a ^ 1) for a in range(group)]

    def step(x, pairs):
        return lax.ppermute(x, axes, pairs)

    def by_near(x):
        return lax.ppermute(x, "chan", near_pairs)

    def by_far(x):
        return lax.ppermute(x, "chan", far_pairs)

    def sib(x):
        return lax.ppermute(x, "chan", other)

    end = (z == 0) | (z == members - 1)
    low = z < members // 2
    mine, theirs = core * part, (1 - core) * part
    starts = [(z ^ 1) * width, jnp.where(low, 2, 1) * width, jnp.where(low, 3, 0) * width]
    table = [chip, chip ^ (1 + core), chip ^ (2 - core), chip ^ 3] + [z * width] + [n + mine for n in starts] + [n + theirs for n in starts]
    table = jnp.stack(table).astype(jnp.int32)
    own_column, columns, other_columns = 4, (5, 6, 7), (8, 9, 10)

    def quarter(n, x):
        return (n, [(0, x)])

    def own_rows(channel):
        rows = lax.dynamic_slice(interaction, (channel, 0, core * part), (1, depth, part))
        return rows.reshape(depth, part)

    (own,) = after([own_rows(chip)], [])
    p1, p2 = step(own, outer), step(own, middle)
    other_t = sib(t_pp)
    fence = sib(own[:16])
    meta = meta_got(meta_over(meta_sent(fence)))
    (meta,) = after([meta], [own])

    (p2,) = after([p2], [meta])
    p1, other_t = after([p1, other_t], [p2])
    p3, near1, far1, p4 = step(p2, outwards), by_near(p1), by_far(p1), step(p1, middle)
    other_meta = sib(meta)
    local = Group([(channel, interaction) for channel in range(channels)], column=own_column)
    ((out,),) = products(table, [t_pp], [meta], [local], [p1], result=shape)

    p3, other_meta = after([p3, other_meta], [out])
    s2 = jnp.where(end, p3, p2)
    far2, near2 = by_far(s2), by_near(s2)
    near1, far1 = after([near1, far1], [s2])
    (p4,) = after([p4], [far1])
    p5 = step(p4, outwards)
    t_rows = [t_pp, other_t]
    metas = [meta, other_meta]
    (sum1,) = products(table, t_rows, metas, [Group([quarter(0, p1), quarter(1, near1), quarter(2, far1)])], [p4])

    (later,) = after([table], [sum1[0]])
    (extra,) = after([own_rows(later[3])], [sum1[0]])
    far2, near2 = after([far2, near2], [extra])
    across2 = by_near(far2)
    (p5,) = after([p5], [far2])
    (extra,) = after([extra], [p5])
    e = step(extra, outer)
    s3 = jnp.where(end, p5, p4)
    far3, near3 = by_far(s3), by_near(s3)
    sum2, sum3 = products(
        table, t_rows, metas,
        [Group([quarter(0, s2), quarter(1, near2), quarter(2, far2)]), Group([quarter(0, s3)])],
        [s3],
    )
    (across2,) = after([across2], [sum2[0]])
    ((out, rest2),) = products(
        table, t_rows, metas, [Group([quarter(3, across2)], before=sum2, column=columns[1])],
        [across2], out=out, result=shape,
    )
    (back2,) = after([sib(rest2)], [out])

    far3, near3 = after([far3, near3], [back2])
    across3 = by_near(far3)
    (e,) = after([e], [near3])
    sum3, (out, rest1) = products(
        table, t_rows, metas,
        [
            Group([quarter(1, near3), quarter(2, far3)], before=sum3),
            Group([quarter(3, e)], before=sum1, column=columns[0]),
        ],
        [e], out=out, result=shape,
    )
    back1, back3 = after([sib(rest1), sib(sum3[1])], [out])

    (across3,) = after([across3], [back3])
    groups = [
        Group([quarter(3, across3)], before=[sum3[0]], column=columns[2]),
        Group([quarter(3, sib(across3))], before=[back3], column=other_columns[2]),
        Group([], before=[back1], column=other_columns[0]),
        Group([], before=[back2], column=other_columns[1]),
    ]
    ((out,), *_) = products(table, [t_pp], [meta], groups, [], out=out, result=shape)
    return out


def on_device(t_pp, interaction, send_order, recv_order, ph_channel, recouple_weight):
    sent = functools.partial(meta_to_send, recv_order, ph_channel, recouple_weight)
    got = functools.partial(meta_of_rows, send_order)
    planes = lax.axis_size("chan") // 2
    if planes == 4 and lax.axis_size("int") == 4 and interaction.shape[0] == planes:
        return grid_plan(t_pp, interaction, sent, meta_over, got)
    return general_plan(t_pp, interaction, got(meta_over(sent())))


def solution(mesh):
    in_specs = (
        P(("chan", "int"), None),
        P(None, None, "int"),
        P(("chan", "int")),
        P(("chan", "int")),
        P("chan"),
        P("chan"),
    )
    out_specs = P(("chan", "int"), None)
    return jax.shard_map(
        on_device, mesh=mesh, in_specs=in_specs, out_specs=out_specs, check_vma=False
    )
```
